32 devices in a mesh: gx: 8 (over z, core), gy: 4 (over y, x).
Axes of the slice: x: 2, y: 2, z: 4, core: 2. Of those that a mesh axis runs over, the one named last changes fastest.
Arguments:
- fields: float32 [2, 512, 1024], P(None, 'gy', 'gx'), may hold values from -8 to 8
- material: int32 [512, 1024], P('gy', 'gx'), may hold values from 0 to 7
- conduct: float32 [2, 8], replicated, may hold values from 0.25 to 4
- joints_x: int32 [512, 8], P('gy'), may hold values from 1 to 1023
- joints_y: int32 [1024, 8], P('gx'), may hold values from 1 to 511
Outputs:
- half_step: float32 [2, 512, 1024], P(None, 'gy', 'gx')
- advanced: float32 [2, 512, 1024], P(None, 'gy', 'gx')
The draws below stay inside these ranges and needn't reach their ends.
Inputs may be any that keep to these rules, and one draw needn't show every extreme that they name: `joints_x`: entries of one row may repeat. `joints_y`: entries of one column may repeat.
All inputs are finite; a program needn't handle non-finite values.
Results may differ from the reference program's by a relative error of at most 0.0015.
Values sent between devices are 32-bit elements; how exact they have to be, the bound alone decides.
A program may use at most 64 MiB of HBM per device.

```python
import math
import jax
import jax.numpy as jnp
from jax import lax

JOINTS = 8
MATERIALS = 8
FOURIER = 8192
DRYING = 4096
NX = 1024
NY = 512


def draw_fields(key, part):
    key_noise, key_region = jax.random.split(key, 2)
    noise_part = jax.random.normal(key_noise, (2, NY, NX), jnp.float32)
    region = jax.random.normal(key_region, (2, 16, 16), jnp.float32) * 2.0
    region = jnp.repeat(jnp.repeat(region, NY // 16, axis=1), NX // 16, axis=2)
    return jnp.clip(noise_part + region, -8.0, 8.0)


def place_ends(result, stream_key, smallest, top_value):
    index_at = [jax.random.randint(jax.random.fold_in(stream_key, axis), (), 0, length) for axis, length in enumerate(result.shape)]
    widest = result.shape.index(max(result.shape))
    next_to = index_at[:widest] + [(index_at[widest] + 1) % result.shape[widest]] + index_at[widest + 1:]
    return result.at[tuple(index_at)].set(smallest).at[tuple(next_to)].set(top_value)


def setup_inputs(seed: int = 0) -> dict:
    streams_of = jax.random.split(jax.random.key(seed), 6)
    return {
        "fields": draw_fields(jax.random.fold_in(streams_of[5], 71), 0),
        "material": place_ends(jax.random.randint(streams_of[1], (NY, NX), 0, MATERIALS), jax.random.fold_in(streams_of[1], 1), 0, MATERIALS - 1).astype(jnp.int32),
        "conduct": jnp.clip(jnp.exp(jax.random.uniform(streams_of[2], (2, MATERIALS), jnp.float32, math.log(0.25), math.log(4.0))), 0.25, 4.0),
        "joints_x": place_ends(jax.random.randint(streams_of[3], (NY, JOINTS), 1, NX), jax.random.fold_in(streams_of[3], 1), 1, NX - 1).astype(jnp.int32),
        "joints_y": place_ends(jax.random.randint(streams_of[4], (NX, JOINTS), 1, NY), jax.random.fold_in(streams_of[4], 1), 1, NY - 1).astype(jnp.int32),
    }


def line_faces(conduction, cut_mask, face_scale):
    interior = face_scale[:, None, None] * 0.5 * (conduction[:, :, :-1] + conduction[:, :, 1:]) * (1.0 - cut_mask[None, :, 1:])
    border = jnp.zeros((conduction.shape[0], conduction.shape[1], 1), jnp.float32)
    return jnp.concatenate([border, interior, border], axis=2)

def line_solve(face_coef, right_side):
    lower = -face_coef[..., :-1]
    upper = -face_coef[..., 1:]
    diagonal = 1.0 + face_coef[..., :-1] + face_coef[..., 1:]
    return lax.linalg.tridiagonal_solve(lower, diagonal, upper, right_side[..., None])[..., 0]

def reference(fields, material, conduct, joints_x, joints_y):
    conduction = conduct[:, material]
    face_scale = jnp.array([FOURIER, DRYING], jnp.float32)
    cut_x = jnp.zeros((NY, NX), jnp.float32).at[jnp.arange(NY, dtype=jnp.int32)[:, None], joints_x].set(1.0)
    cut_y = jnp.zeros((NX, NY), jnp.float32).at[jnp.arange(NX, dtype=jnp.int32)[:, None], joints_y].set(1.0)
    half_step = line_solve(line_faces(conduction, cut_x, face_scale), fields)
    turned = jnp.transpose(conduction, (0, 2, 1))
    advanced = line_solve(line_faces(turned, cut_y, face_scale), jnp.transpose(half_step, (0, 2, 1)))
    return (half_step, jnp.transpose(advanced, (0, 2, 1)))
```

```python
import functools

import jax
import jax.numpy as jnp
from jax import lax
from jax.experimental import pallas as pl
from jax.experimental.pallas import tpu as pltpu
from jax.sharding import PartitionSpec as P

MATERIALS = 8
FOURIER = 8192
DRYING = 4096
SCALES = (0.5 * FOURIER, 0.5 * DRYING)
SUB = 8
SLOT = 16
ROWS = 14


def lookup(conduct, comp, mats):
    low, mid, high = mats
    v = [conduct[comp, k] for k in range(MATERIALS)]
    pair = [jnp.where(low, v[2 * k + 1], v[2 * k]) for k in range(4)]
    quad = [jnp.where(mid, pair[2 * k + 1], pair[2 * k]) for k in range(2)]
    return jnp.where(high, quad[1], quad[0])


def fold(links, ground):
    ground = list(ground)
    index = list(range(len(ground)))
    plan = []
    while len(index) > 2:
        keep, merged = [index[0]], []
        p = 1
        while p < len(index):
            if p + 1 < len(index):
                a, k, b = index[p - 1 : p + 2]
                w = 1.0 / (links[p - 1] + links[p] + ground[k])
                lo, hi = links[p - 1] * w, links[p] * w
                merged.append(links[p - 1] * hi)
                ground[a] = ground[a] + lo * ground[k]
                ground[b] = ground[b] + hi * ground[k]
                plan.append((a, k, b, lo, hi, w))
                keep.append(b)
                p += 2
            else:
                merged.append(links[p - 1])
                keep.append(index[p])
                p += 1
        index, links = keep, merged
    return plan, links[0], ground[0], ground[-1]


def fold_source(plan, source):
    source = list(source)
    for a, k, b, lo, hi, _ in plan:
        source[a] = source[a] + lo * source[k]
        source[b] = source[b] + hi * source[k]
    return source


def unfold(plan, source, first, last):
    x = {0: first, len(source) - 1: last}
    for a, k, b, lo, hi, w in reversed(plan):
        x[k] = source[k] * w + lo * x[a] + hi * x[b]
    return [x[k] for k in range(len(source))]


def roll(x, shift):
    return pltpu.roll(x, shift % x.shape[0], 0)


def block_structure(conduct, mat_ref, joints, base):
    span = mat_ref.shape[0] // SUB
    lane = mat_ref.shape[1]
    sub = lax.broadcasted_iota(jnp.int32, (SUB, lane), 0)
    bits = jnp.zeros((SUB, lane), jnp.int32)
    for k in range(joints.shape[0]):
        at = joints[k : k + 1, :] - base - sub * span
        bits = bits | jnp.where(
            (at >= 1) & (at <= span), jnp.left_shift(1, jnp.clip(at, 0, span)), 0
        )
    masks = []
    for t in range(span):
        mat = mat_ref[pl.ds(t, SUB, stride=span), :]
        masks.append(((mat & 1) != 0, (mat & 2) != 0, (mat & 4) != 0))
    cut = [(bits & (1 << (t + 1))) != 0 for t in range(span)]
    out = []
    for comp in range(2):
        cond = [lookup(conduct, comp, m) for m in masks]
        after = cond[1:] + [roll(cond[0], -1)]
        face = [
            jnp.where(cut[t], 0.0, SCALES[comp] * (cond[t] + after[t])) for t in range(span)
        ]
        ones = jnp.ones((SUB, lane), jnp.float32)
        plan, b, gp, gq = fold(face[:-1], [ones] * span)
        link = jnp.where(sub == SUB - 1, 0.0, face[-1])
        wq = 1.0 / (b + link + gq)
        lo = jnp.where(sub == SUB - 1, 0.0, b * wq)
        hi = link * wq
        c = jnp.where(sub == SUB - 1, b, b * hi)
        a = jnp.where(sub == 0, 0.0, roll(c, 1))
        g = gp + lo * gq + roll(hi * gq, 1)
        g_first = g
        steps = []
        s = 1
        while s < SUB:
            w = 1.0 / (a + c + g)
            right = jnp.where((sub >= 1) & (sub <= SUB - 1 - s), c * w, 0.0)
            left = jnp.where(sub >= 1 + s, a * w, 0.0)
            steps.append((s, right, left))
            g_new = g + roll(right * g, s) + roll(left * g, -s)
            a_new = jnp.where(sub >= 1 + s, roll(right * a, s), a)
            c_new = jnp.where(sub <= SUB - 1 - s, roll(left * c, -s), c)
            a, c, g = a_new, c_new, g_new
            s *= 2
        w = 1.0 / (a + c + g)
        aw, cw = a * w, c * w
        between = (aw * c)[1:2, :]
        ground0 = g_first[0:1, :] + (aw * g)[1:2, :]
        ground1 = (gq + cw * g)[SUB - 1 : SUB, :]
        cond0 = cond[0][0:1, :]
        cond1 = cond[-1][SUB - 1 : SUB, :]
        inner = dict(
            plan=plan, b=b, link=link, wq=wq, lo=lo, hi=hi, steps=steps, w=w, aw=aw, cw=cw
        )
        out.append((inner, (between, ground0, ground1, cond0, cond1)))
    return out


def block_source(inner, source):
    source = fold_source(inner["plan"], source)
    fq = source[-1]
    f = source[0] + inner["lo"] * fq + roll(inner["hi"] * fq, 1)
    f_first = f
    for s, right, left in inner["steps"]:
        f = f + roll(right * f, s) + roll(left * f, -s)
    f0 = f_first[0:1, :] + (inner["aw"] * f)[1:2, :]
    f1 = (fq + inner["cw"] * f)[SUB - 1 : SUB, :]
    return (source, f), f0, f1


def block_solve(inner, kept, first, last):
    source, f = kept
    sub = lax.broadcasted_iota(jnp.int32, f.shape, 0)
    xp = f * inner["w"] + inner["aw"] * first + inner["cw"] * last
    xp = jnp.where(sub == 0, first, xp)
    xq = (source[-1] + inner["b"] * xp + inner["link"] * roll(xp, -1)) * inner["wq"]
    xq = jnp.where(sub == SUB - 1, last, xq)
    return unfold(inner["plan"], source, xp, xq)


def chain_solve(comp, held, joints, count, block):
    slots = held.shape[0] // SLOT

    def item(q):
        return held[pl.ds(7 * comp + q, slots, stride=SLOT), :]

    b, g0, g1, k0, k1, f0, f1 = [item(q) for q in range(7)]
    pos = lax.broadcasted_iota(jnp.int32, b.shape, 0)
    cut = pos >= count - 1
    for k in range(joints.shape[0]):
        cut = cut | (joints[k : k + 1, :] == (pos + 1) * block)
    link = jnp.where(cut, 0.0, SCALES[comp] * (k1 + roll(k0, -1)))
    wr = 1.0 / (b + link + g1)
    lo, hi = b * wr, link * wr
    c = b * hi
    a = roll(c, 1)
    g = g0 + lo * g1 + roll(hi * g1, 1)
    f = f0 + lo * f1 + roll(hi * f1, 1)
    s = 1
    while s < count:
        w = 1.0 / (a + c + g)
        right, left = c * w, a * w
        f = f + roll(right * f, s) + roll(left * f, -s)
        g_new = g + roll(right * g, s) + roll(left * g, -s)
        a, c, g = roll(right * a, s), roll(left * c, -s), g_new
        s *= 2
    x0 = f / g
    x1 = (f1 + b * x0 + link * roll(x0, -1)) * wr
    return x0, x1


def kernel(
    fields, material, conduct, joints_x, joints_y, half, advanced,
    field_t, mat_t, half_t, held_x, held_y, ends,
    send_x, recv_x, send_y, recv_y,
):
    nx, ny = lax.axis_size("gx"), lax.axis_size("gy")
    mx, my = lax.axis_index("gx"), lax.axis_index("gy")
    rows, cols = material.shape
    axes = (("gx", nx, mx, held_x, send_x, recv_x), ("gy", ny, my, held_y, send_y, recv_y))

    barrier = pltpu.get_barrier_semaphore()
    for axis, n, me, _, _, _ in axes:
        for off in range(1, n):
            pl.semaphore_signal(
                barrier, inc=1, device_id={axis: lax.rem(me + off, n)},
                device_id_type=pl.DeviceIdType.MESH,
            )

    for axis, n, me, held, _, _ in axes:
        slots = held.shape[0] // SLOT
        if slots > n:
            held[n * SLOT :, :] = jnp.ones(((slots - n) * SLOT, cols), jnp.float32)

    def copy_to(which, off):
        axis, n, me, held, send, recv = axes[which]
        peer = lax.rem(me + off, n)
        own = held.at[pl.ds(pl.multiple_of(me * SLOT, SLOT), SLOT), :]
        return pltpu.make_async_remote_copy(
            src_ref=own, dst_ref=own, send_sem=send.at[off], recv_sem=recv.at[me],
            device_id={axis: peer}, device_id_type=pl.DeviceIdType.MESH,
        )

    def copy_from(which, off):
        axis, n, me, held, send, recv = axes[which]
        peer = lax.rem(me + off, n)
        theirs = held.at[pl.ds(pl.multiple_of(peer * SLOT, SLOT), SLOT), :]
        return pltpu.make_async_remote_copy(
            src_ref=theirs, dst_ref=theirs, send_sem=send.at[off], recv_sem=recv.at[peer],
            device_id={axis: peer}, device_id_type=pl.DeviceIdType.MESH,
        )

    def publish(which, parts):
        _, n, me, held, _, _ = axes[which]
        lines = [row for part in parts for row in part]
        lines += [jnp.zeros_like(lines[0])] * (SLOT - len(lines))
        held[pl.ds(pl.multiple_of(me * SLOT, SLOT), SLOT), :] = jnp.concatenate(lines, axis=0)

    def gather_ends(which, joints, block):
        _, n, me, held, _, _ = axes[which]
        slots = held.shape[0] // SLOT
        found = []
        for comp in range(2):
            x0, x1 = chain_solve(comp, held, joints, n, block)
            ends[pl.ds(0, slots), :] = x0
            ends[pl.ds(slots, slots), :] = x1
            found.append((ends[pl.ds(me, 1), :], ends[pl.ds(me + slots, 1), :]))
        return found

    mat_t[...] = material[...].T
    for comp in range(2):
        field_t[comp] = fields[comp].T
    jx, jy = joints_x[...], joints_y[...]

    span = cols // SUB
    along_x = block_structure(conduct, mat_t, jx, mx * cols)
    kept_x, parts = [], []
    for comp in range(2):
        inner, shared = along_x[comp]
        kept, f0, f1 = block_source(
            inner, [field_t[comp, pl.ds(t, SUB, stride=span), :] for t in range(span)]
        )
        kept_x.append(kept)
        parts.append(shared + (f0, f1))
    publish(0, parts)
    pl.semaphore_wait(barrier, nx + ny - 2)
    for off in range(1, nx):
        copy_to(0, off).start()
    span_y = rows // SUB
    along_y = block_structure(conduct, material, jy, my * rows)
    for off in range(1, nx):
        copy_from(0, off).wait_recv()
    found = gather_ends(0, jx, cols)
    for comp in range(2):
        x = block_solve(along_x[comp][0], kept_x[comp], *found[comp])
        for t in range(span):
            half_t[comp, pl.ds(t, SUB, stride=span), :] = x[t]
        half[comp] = half_t[comp].T

    kept_y, parts = [], []
    for comp in range(2):
        inner, shared = along_y[comp]
        kept, f0, f1 = block_source(
            inner, [half[comp, pl.ds(t, SUB, stride=span_y), :] for t in range(span_y)]
        )
        kept_y.append(kept)
        parts.append(shared + (f0, f1))
    publish(1, parts)
    for off in range(1, ny):
        copy_to(1, off).start()
    for off in range(1, ny):
        copy_from(1, off).wait_recv()
    found = gather_ends(1, jy, rows)
    for comp in range(2):
        x = block_solve(along_y[comp][0], kept_y[comp], *found[comp])
        for t in range(span_y):
            advanced[comp, pl.ds(t, SUB, stride=span_y), :] = x[t]
    for off in range(1, nx):
        copy_to(0, off).wait_send()
    for off in range(1, ny):
        copy_to(1, off).wait_send()


def per_device(nx, ny, fields, material, conduct, joints_x, joints_y):
    rows, cols = material.shape
    vmem = pl.BlockSpec(memory_space=pltpu.VMEM)
    shape = jax.ShapeDtypeStruct(fields.shape, jnp.float32)
    sx, sy = max(nx, SUB), max(ny, SUB)
    return pl.pallas_call(
        kernel,
        out_shape=(shape, shape),
        in_specs=[vmem, vmem, pl.BlockSpec(memory_space=pltpu.SMEM), vmem, vmem],
        out_specs=(vmem, vmem),
        scratch_shapes=[
            pltpu.VMEM((2, cols, rows), jnp.float32),
            pltpu.VMEM((cols, rows), jnp.int32),
            pltpu.VMEM((2, cols, rows), jnp.float32),
            pltpu.VMEM((sx * SLOT, rows), jnp.float32),
            pltpu.VMEM((sy * SLOT, cols), jnp.float32),
            pltpu.VMEM((2 * max(sx, sy), cols), jnp.float32),
            pltpu.SemaphoreType.DMA((nx,)),
            pltpu.SemaphoreType.DMA((nx,)),
            pltpu.SemaphoreType.DMA((ny,)),
            pltpu.SemaphoreType.DMA((ny,)),
        ],
        compiler_params=pltpu.CompilerParams(
            collective_id=0, has_side_effects=True, vmem_limit_bytes=16 * 1024 * 1024
        ),
    )(fields, material, conduct, joints_x.T, joints_y.T)


def solution(mesh):
    return jax.shard_map(
        functools.partial(per_device, mesh.shape["gx"], mesh.shape["gy"]),
        mesh=mesh,
        in_specs=(P(None, "gy", "gx"), P("gy", "gx"), P(), P("gy", None), P("gx", None)),
        out_specs=(P(None, "gy", "gx"), P(None, "gy", "gx")),
        check_vma=False,
    )
```

```python
import functools

import jax
import jax.numpy as jnp
from jax import lax
from jax.experimental import pallas as pl
from jax.experimental.pallas import tpu as pltpu
from jax.sharding import PartitionSpec as P

MATERIALS = 8
FOURIER = 8192
DRYING = 4096
SCALES = (0.5 * FOURIER, 0.5 * DRYING)
SUB = 8
SLOT = 16
ROWS = 14


def lookup(conduct, comp, mats):
    low, mid, high = mats
    v = [conduct[comp, k] for k in range(MATERIALS)]
    pair = [jnp.where(low, v[2 * k + 1], v[2 * k]) for k in range(4)]
    quad = [jnp.where(mid, pair[2 * k + 1], pair[2 * k]) for k in range(2)]
    return jnp.where(high, quad[1], quad[0])


def fold(links, ground):
    ground = list(ground)
    index = list(range(len(ground)))
    plan = []
    while len(index) > 2:
        keep, merged = [index[0]], []
        p = 1
        while p < len(index):
            if p + 1 < len(index):
                a, k, b = index[p - 1 : p + 2]
                w = 1.0 / (links[p - 1] + links[p] + ground[k])
                lo, hi = links[p - 1] * w, links[p] * w
                merged.append(links[p - 1] * hi)
                ground[a] = ground[a] + lo * ground[k]
                ground[b] = ground[b] + hi * ground[k]
                plan.append((a, k, b, lo, hi, w))
                keep.append(b)
                p += 2
            else:
                merged.append(links[p - 1])
                keep.append(index[p])
                p += 1
        index, links = keep, merged
    return plan, links[0], ground[0], ground[-1]


def fold_source(plan, source):
    source = list(source)
    for a, k, b, lo, hi, _ in plan:
        source[a] = source[a] + lo * source[k]
        source[b] = source[b] + hi * source[k]
    return source


def unfold(plan, source, first, last):
    x = {0: first, len(source) - 1: last}
    for a, k, b, lo, hi, w in reversed(plan):
        x[k] = source[k] * w + lo * x[a] + hi * x[b]
    return [x[k] for k in range(len(source))]


def roll(x, shift):
    return pltpu.roll(x, shift % x.shape[0], 0)


def block_structure(conduct, mat_ref, joints, base):
    span = mat_ref.shape[0] // SUB
    lane = mat_ref.shape[1]
    sub = lax.broadcasted_iota(jnp.int32, (SUB, lane), 0)
    bits = jnp.zeros((SUB, lane), jnp.int32)
    for k in range(joints.shape[0]):
        at = joints[k : k + 1, :] - base - sub * span
        bits = bits | jnp.where(
            (at >= 1) & (at <= span), jnp.left_shift(1, jnp.clip(at, 0, span)), 0
        )
    masks = []
    for t in range(span):
        mat = mat_ref[pl.ds(t, SUB, stride=span), :]
        masks.append(((mat & 1) != 0, (mat & 2) != 0, (mat & 4) != 0))
    cut = [(bits & (1 << (t + 1))) != 0 for t in range(span)]
    out = []
    for comp in range(2):
        cond = [lookup(conduct, comp, m) for m in masks]
        after = cond[1:] + [roll(cond[0], -1)]
        face = [
            jnp.where(cut[t], 0.0, SCALES[comp] * (cond[t] + after[t])) for t in range(span)
        ]
        ones = jnp.ones((SUB, lane), jnp.float32)
        plan, b, gp, gq = fold(face[:-1], [ones] * span)
        link = jnp.where(sub == SUB - 1, 0.0, face[-1])
        wq = 1.0 / (b + link + gq)
        lo = jnp.where(sub == SUB - 1, 0.0, b * wq)
        hi = link * wq
        c = jnp.where(sub == SUB - 1, b, b * hi)
        a = jnp.where(sub == 0, 0.0, roll(c, 1))
        g = gp + lo * gq + roll(hi * gq, 1)
        g_first = g
        steps = []
        s = 1
        while s < SUB:
            w = 1.0 / (a + c + g)
            right = jnp.where((sub >= 1) & (sub <= SUB - 1 - s), c * w, 0.0)
            left = jnp.where(sub >= 1 + s, a * w, 0.0)
            steps.append((s, right, left))
            g_new = g + roll(right * g, s) + roll(left * g, -s)
            a_new = jnp.where(sub >= 1 + s, roll(right * a, s), a)
            c_new = jnp.where(sub <= SUB - 1 - s, roll(left * c, -s), c)
            a, c, g = a_new, c_new, g_new
            s *= 2
        w = 1.0 / (a + c + g)
        aw, cw = a * w, c * w
        between = (aw * c)[1:2, :]
        ground0 = g_first[0:1, :] + (aw * g)[1:2, :]
        ground1 = (gq + cw * g)[SUB - 1 : SUB, :]
        cond0 = cond[0][0:1, :]
        cond1 = cond[-1][SUB - 1 : SUB, :]
        inner = dict(
            plan=plan, b=b, link=link, wq=wq, lo=lo, hi=hi, steps=steps, w=w, aw=aw, cw=cw
        )
        out.append((inner, (between, ground0, ground1, cond0, cond1)))
    return out


def block_source(inner, source):
    source = fold_source(inner["plan"], source)
    fq = source[-1]
    f = source[0] + inner["lo"] * fq + roll(inner["hi"] * fq, 1)
    f_first = f
    for s, right, left in inner["steps"]:
        f = f + roll(right * f, s) + roll(left * f, -s)
    f0 = f_first[0:1, :] + (inner["aw"] * f)[1:2, :]
    f1 = (fq + inner["cw"] * f)[SUB - 1 : SUB, :]
    return (source, f), f0, f1


def block_solve(inner, kept, first, last):
    source, f = kept
    sub = lax.broadcasted_iota(jnp.int32, f.shape, 0)
    xp = f * inner["w"] + inner["aw"] * first + inner["cw"] * last
    xp = jnp.where(sub == 0, first, xp)
    xq = (source[-1] + inner["b"] * xp + inner["link"] * roll(xp, -1)) * inner["wq"]
    xq = jnp.where(sub == SUB - 1, last, xq)
    return unfold(inner["plan"], source, xp, xq)


def chain_solve(comp, held, joints, count, block):
    slots = held.shape[0] // SLOT

    def item(q):
        return held[pl.ds(7 * comp + q, slots, stride=SLOT), :]

    b, g0, g1, k0, k1, f0, f1 = [item(q) for q in range(7)]
    pos = lax.broadcasted_iota(jnp.int32, b.shape, 0)
    cut = pos >= count - 1
    for k in range(joints.shape[0]):
        cut = cut | (joints[k : k + 1, :] == (pos + 1) * block)
    link = jnp.where(cut, 0.0, SCALES[comp] * (k1 + roll(k0, -1)))
    wr = 1.0 / (b + link + g1)
    lo, hi = b * wr, link * wr
    c = b * hi
    a = roll(c, 1)
    g = g0 + lo * g1 + roll(hi * g1, 1)
    f = f0 + lo * f1 + roll(hi * f1, 1)
    s = 1
    while s < count:
        w = 1.0 / (a + c + g)
        right, left = c * w, a * w
        f = f + roll(right * f, s) + roll(left * f, -s)
        g_new = g + roll(right * g, s) + roll(left * g, -s)
        a, c, g = roll(right * a, s), roll(left * c, -s), g_new
        s *= 2
    x0 = f / g
    x1 = (f1 + b * x0 + link * roll(x0, -1)) * wr
    return x0, x1


def kernel(
    fields_in, material_in, conduct_in, joints_x_in, joints_y_in, half, advanced,
    fields, material, conduct, joints_x, joints_y,
    field_t, mat_t, half_t, held_x, held_y, ends,
    send_x, recv_x, send_y, recv_y, load_sem,
):
    nx, ny = lax.axis_size("gx"), lax.axis_size("gy")
    mx, my = lax.axis_index("gx"), lax.axis_index("gy")
    rows, cols = material.shape
    axes = (("gx", nx, mx, held_x, send_x, recv_x), ("gy", ny, my, held_y, send_y, recv_y))

    barrier = pltpu.get_barrier_semaphore()
    for axis, n, me, _, _, _ in axes:
        for off in range(1, n):
            pl.semaphore_signal(
                barrier, inc=1, device_id={axis: lax.rem(me + off, n)},
                device_id_type=pl.DeviceIdType.MESH,
            )

    loads = [
        pltpu.make_async_copy(source, target, load_sem.at[i])
        for i, (source, target) in enumerate(
            (
                (material_in, material),
                (conduct_in, conduct),
                (joints_x_in, joints_x),
                (fields_in, fields),
                (joints_y_in, joints_y),
            )
        )
    ]
    for load in loads:
        load.start()

    for axis, n, me, held, _, _ in axes:
        slots = held.shape[0] // SLOT
        if slots > n:
            held[n * SLOT :, :] = jnp.ones(((slots - n) * SLOT, cols), jnp.float32)

    def copy_to(which, off):
        axis, n, me, held, send, recv = axes[which]
        peer = lax.rem(me + off, n)
        own = held.at[pl.ds(pl.multiple_of(me * SLOT, SLOT), SLOT), :]
        return pltpu.make_async_remote_copy(
            src_ref=own, dst_ref=own, send_sem=send.at[off], recv_sem=recv.at[me],
            device_id={axis: peer}, device_id_type=pl.DeviceIdType.MESH,
        )

    def copy_from(which, off):
        axis, n, me, held, send, recv = axes[which]
        peer = lax.rem(me + off, n)
        theirs = held.at[pl.ds(pl.multiple_of(peer * SLOT, SLOT), SLOT), :]
        return pltpu.make_async_remote_copy(
            src_ref=theirs, dst_ref=theirs, send_sem=send.at[off], recv_sem=recv.at[peer],
            device_id={axis: peer}, device_id_type=pl.DeviceIdType.MESH,
        )

    def publish(which, parts):
        _, n, me, held, _, _ = axes[which]
        lines = [row for part in parts for row in part]
        lines += [jnp.zeros_like(lines[0])] * (SLOT - len(lines))
        held[pl.ds(pl.multiple_of(me * SLOT, SLOT), SLOT), :] = jnp.concatenate(lines, axis=0)

    def gather_ends(which, joints, block):
        _, n, me, held, _, _ = axes[which]
        slots = held.shape[0] // SLOT
        found = []
        for comp in range(2):
            x0, x1 = chain_solve(comp, held, joints, n, block)
            ends[pl.ds(0, slots), :] = x0
            ends[pl.ds(slots, slots), :] = x1
            found.append((ends[pl.ds(me, 1), :], ends[pl.ds(me + slots, 1), :]))
        return found

    for load in loads[:4]:
        load.wait()
    mat_t[...] = material[...].T
    for comp in range(2):
        field_t[comp] = fields[comp].T
    jx = joints_x[...]

    span = cols // SUB
    along_x = block_structure(conduct, mat_t, jx, mx * cols)
    kept_x, parts = [], []
    for comp in range(2):
        inner, shared = along_x[comp]
        kept, f0, f1 = block_source(
            inner, [field_t[comp, pl.ds(t, SUB, stride=span), :] for t in range(span)]
        )
        kept_x.append(kept)
        parts.append(shared + (f0, f1))
    publish(0, parts)
    pl.semaphore_wait(barrier, nx + ny - 2)
    for off in range(1, nx):
        copy_to(0, off).start()
    loads[4].wait()
    jy = joints_y[...]
    span_y = rows // SUB
    along_y = block_structure(conduct, material, jy, my * rows)
    for off in range(1, nx):
        copy_from(0, off).wait_recv()
    found = gather_ends(0, jx, cols)
    for comp in range(2):
        x = block_solve(along_x[comp][0], kept_x[comp], *found[comp])
        for t in range(span):
            half_t[comp, pl.ds(t, SUB, stride=span), :] = x[t]
        half[comp] = half_t[comp].T

    kept_y, parts = [], []
    for comp in range(2):
        inner, shared = along_y[comp]
        kept, f0, f1 = block_source(
            inner, [half[comp, pl.ds(t, SUB, stride=span_y), :] for t in range(span_y)]
        )
        kept_y.append(kept)
        parts.append(shared + (f0, f1))
    publish(1, parts)
    for off in range(1, ny):
        copy_to(1, off).start()
    for off in range(1, ny):
        copy_from(1, off).wait_recv()
    found = gather_ends(1, jy, rows)
    for comp in range(2):
        x = block_solve(along_y[comp][0], kept_y[comp], *found[comp])
        for t in range(span_y):
            advanced[comp, pl.ds(t, SUB, stride=span_y), :] = x[t]
    for off in range(1, nx):
        copy_to(0, off).wait_send()
    for off in range(1, ny):
        copy_to(1, off).wait_send()


def write_out(half, advanced, half_out, advanced_out, sems):
    copies = [
        pltpu.make_async_copy(half, half_out, sems.at[0]),
        pltpu.make_async_copy(advanced, advanced_out, sems.at[1]),
    ]
    for copy in copies:
        copy.start()
    for copy in copies:
        copy.wait()


def per_device(nx, ny, fields, material, conduct, joints_x, joints_y):
    rows, cols = material.shape
    joints = joints_x.shape[1]
    vmem = pl.BlockSpec(memory_space=pltpu.VMEM)
    hbm = pl.BlockSpec(memory_space=pltpu.HBM)
    shape = jax.ShapeDtypeStruct(fields.shape, jnp.float32)
    sx, sy = max(nx, SUB), max(ny, SUB)
    solved = pl.pallas_call(
        kernel,
        out_shape=(shape, shape),
        in_specs=[hbm] * 5,
        out_specs=(vmem, vmem),
        scratch_shapes=[
            pltpu.VMEM((2, rows, cols), jnp.float32),
            pltpu.VMEM((rows, cols), jnp.int32),
            pltpu.SMEM(conduct.shape, jnp.float32),
            pltpu.VMEM((joints, rows), jnp.int32),
            pltpu.VMEM((joints, cols), jnp.int32),
            pltpu.VMEM((2, cols, rows), jnp.float32),
            pltpu.VMEM((cols, rows), jnp.int32),
            pltpu.VMEM((2, cols, rows), jnp.float32),
            pltpu.VMEM((sx * SLOT, rows), jnp.float32),
            pltpu.VMEM((sy * SLOT, cols), jnp.float32),
            pltpu.VMEM((2 * max(sx, sy), cols), jnp.float32),
            pltpu.SemaphoreType.DMA((nx,)),
            pltpu.SemaphoreType.DMA((nx,)),
            pltpu.SemaphoreType.DMA((ny,)),
            pltpu.SemaphoreType.DMA((ny,)),
            pltpu.SemaphoreType.DMA((5,)),
        ],
        compiler_params=pltpu.CompilerParams(
            collective_id=0, has_side_effects=True, vmem_limit_bytes=16 * 1024 * 1024
        ),
    )(
        *(
            pltpu.with_memory_space_constraint(x, pltpu.HBM)
            for x in (fields, material, conduct, joints_x.T, joints_y.T)
        )
    )
    return pl.pallas_call(
        write_out,
        out_shape=(shape, shape),
        in_specs=[vmem, vmem],
        out_specs=(hbm, hbm),
        scratch_shapes=[pltpu.SemaphoreType.DMA((2,))],
        compiler_params=pltpu.CompilerParams(vmem_limit_bytes=4 * 1024 * 1024),
    )(*solved)


def solution(mesh):
    return jax.shard_map(
        functools.partial(per_device, mesh.shape["gx"], mesh.shape["gy"]),
        mesh=mesh,
        in_specs=(P(None, "gy", "gx"), P("gy", "gx"), P(), P("gy", None), P("gx", None)),
        out_specs=(P(None, "gy", "gx"), P(None, "gy", "gx")),
        check_vma=False,
    )
```

```python
import functools

import jax
import jax.numpy as jnp
from jax import lax
from jax.experimental import pallas as pl
from jax.experimental.pallas import tpu as pltpu
from jax.sharding import PartitionSpec as P

MATERIALS = 8
FOURIER = 8192
DRYING = 4096
SCALES = (0.5 * FOURIER, 0.5 * DRYING)
SUB = 8
SLOT = 16
ROWS = 12


def inverse(x):
    guess = pl.reciprocal(x, approx=True)
    return guess * (2.0 - x * guess)


def lookup(conduct, comp, mats):
    low, mid, high = mats
    v = [conduct[comp, k] for k in range(MATERIALS)]
    pair = [jnp.where(low, v[2 * k + 1], v[2 * k]) for k in range(4)]
    quad = [jnp.where(mid, pair[2 * k + 1], pair[2 * k]) for k in range(2)]
    return jnp.where(high, quad[1], quad[0])


def bit_masks(mat):
    return (mat & 1) != 0, (mat & 2) != 0, (mat & 4) != 0


def fold(links, ground):
    ground = list(ground)
    index = list(range(len(ground)))
    plan = []
    while len(index) > 2:
        keep, merged = [index[0]], []
        p = 1
        while p < len(index):
            if p + 1 < len(index):
                a, k, b = index[p - 1 : p + 2]
                w = inverse(links[p - 1] + links[p] + ground[k])
                lo, hi = links[p - 1] * w, links[p] * w
                merged.append(links[p - 1] * hi)
                ground[a] = ground[a] + lo * ground[k]
                ground[b] = ground[b] + hi * ground[k]
                plan.append((a, k, b, lo, hi, w))
                keep.append(b)
                p += 2
            else:
                merged.append(links[p - 1])
                keep.append(index[p])
                p += 1
        index, links = keep, merged
    return plan, links[0], ground[0], ground[-1]


def fold_source(plan, source):
    source = list(source)
    for a, k, b, lo, hi, _ in plan:
        source[a] = source[a] + lo * source[k]
        source[b] = source[b] + hi * source[k]
    return source


def unfold(plan, source, first, last):
    x = {0: first, len(source) - 1: last}
    for a, k, b, lo, hi, w in reversed(plan):
        x[k] = source[k] * w + lo * x[a] + hi * x[b]
    return [x[k] for k in range(len(source))]


def roll(x, shift):
    return pltpu.roll(x, shift % x.shape[0], 0)


def block_structure(conduct, mat_ref, joints, base):
    span = mat_ref.shape[0] // SUB
    lane = mat_ref.shape[1]
    sub = lax.broadcasted_iota(jnp.int32, (SUB, lane), 0)
    bits = jnp.zeros((SUB, lane), jnp.int32)
    for k in range(joints.shape[0]):
        at = joints[k : k + 1, :] - base - sub * span
        bits = bits | jnp.where(
            (at >= 1) & (at <= span), jnp.left_shift(1, jnp.clip(at, 0, span)), 0
        )
    masks = []
    for t in range(span):
        last = mat_ref[pl.ds(t, SUB, stride=span), :]
        first = last if t == 0 else first
        masks.append(bit_masks(last))
    cut = [(bits & (1 << (t + 1))) != 0 for t in range(span)]
    out = []
    for comp in range(2):
        cond = [lookup(conduct, comp, m) for m in masks]
        after = cond[1:] + [roll(cond[0], -1)]
        face = [
            jnp.where(cut[t], 0.0, SCALES[comp] * (cond[t] + after[t])) for t in range(span)
        ]
        ones = jnp.ones((SUB, lane), jnp.float32)
        plan, b, gp, gq = fold(face[:-1], [ones] * span)
        link = jnp.where(sub == SUB - 1, 0.0, face[-1])
        wq = inverse(b + link + gq)
        lo = jnp.where(sub == SUB - 1, 0.0, b * wq)
        hi = link * wq
        c = jnp.where(sub == SUB - 1, b, b * hi)
        a = jnp.where(sub == 0, 0.0, roll(c, 1))
        g = gp + lo * gq + roll(hi * gq, 1)
        g_first = g
        steps = []
        s = 1
        while s < SUB:
            w = inverse(a + c + g)
            right = jnp.where((sub >= 1) & (sub <= SUB - 1 - s), c * w, 0.0)
            left = jnp.where(sub >= 1 + s, a * w, 0.0)
            steps.append((s, right, left))
            g_new = g + roll(right * g, s) + roll(left * g, -s)
            a_new = jnp.where(sub >= 1 + s, roll(right * a, s), a)
            c_new = jnp.where(sub <= SUB - 1 - s, roll(left * c, -s), c)
            a, c, g = a_new, c_new, g_new
            s *= 2
        w = inverse(a + c + g)
        aw, cw = a * w, c * w
        between = (aw * c)[1:2, :]
        ground0 = g_first[0:1, :] + (aw * g)[1:2, :]
        ground1 = (gq + cw * g)[SUB - 1 : SUB, :]
        inner = dict(
            plan=plan, b=b, link=link, wq=wq, lo=lo, hi=hi, steps=steps, w=w, aw=aw, cw=cw
        )
        out.append((inner, (between, ground0, ground1)))
    return out, (first[0:1, :].astype(jnp.float32), last[SUB - 1 : SUB, :].astype(jnp.float32))


def block_source(inner, source):
    source = fold_source(inner["plan"], source)
    fq = source[-1]
    f = source[0] + inner["lo"] * fq + roll(inner["hi"] * fq, 1)
    f_first = f
    for s, right, left in inner["steps"]:
        f = f + roll(right * f, s) + roll(left * f, -s)
    f0 = f_first[0:1, :] + (inner["aw"] * f)[1:2, :]
    f1 = (fq + inner["cw"] * f)[SUB - 1 : SUB, :]
    return (source, f), f0, f1


def block_solve(inner, kept, first, last):
    source, f = kept
    sub = lax.broadcasted_iota(jnp.int32, f.shape, 0)
    xp = f * inner["w"] + inner["aw"] * first + inner["cw"] * last
    xp = jnp.where(sub == 0, first, xp)
    xq = (source[-1] + inner["b"] * xp + inner["link"] * roll(xp, -1)) * inner["wq"]
    xq = jnp.where(sub == SUB - 1, last, xq)
    return unfold(inner["plan"], source, xp, xq)


def chain_structure(conduct, comp, rows, mats, joints, count, block):
    b, g0, g1 = rows
    slots = b.shape[0]
    pos = lax.broadcasted_iota(jnp.int32, b.shape, 0)
    cut = pos >= count - 1
    for k in range(joints.shape[0]):
        cut = cut | (joints[k : k + 1, :] == (pos + 1) * block)
    k0, k1 = [lookup(conduct, comp, bit_masks(m.astype(jnp.int32))) for m in mats]
    link = jnp.where(cut, 0.0, SCALES[comp] * (k1 + roll(k0, -1)))
    wr = inverse(b + link + g1)
    lo, hi = b * wr, link * wr
    c = b * hi
    a = roll(c, 1)
    g = g0 + lo * g1 + roll(hi * g1, 1)
    steps = []
    s = 1
    while s < count:
        w = inverse(a + c + g)
        right, left = c * w, a * w
        steps.append((s, right, left))
        g_new = g + roll(right * g, s) + roll(left * g, -s)
        a, c, g = roll(right * a, s), roll(left * c, -s), g_new
        s *= 2
    return b, link, wr, lo, hi, steps, inverse(g)


def chain_source(structure, f0, f1):
    b, link, wr, lo, hi, steps, w = structure
    f = f0 + lo * f1 + roll(hi * f1, 1)
    for s, right, left in steps:
        f = f + roll(right * f, s) + roll(left * f, -s)
    x0 = f * w
    x1 = (f1 + b * x0 + link * roll(x0, -1)) * wr
    return x0, x1


def far_first(me, n, k):
    down = n - 1 - k - lax.div(me + k + 1, n)
    up = k + lax.div(k - me + n, n)
    half = lax.div(2 * me, n)
    return half * up + (1 - half) * down


def kernel(
    fields_in, material_in, conduct_in, joints_x_in, joints_y_in, half, advanced,
    fields, material, conduct, joints_x, joints_y,
    field_t, mat_t, half_t, held_x, held_y, flow_y, ends,
    send_x, recv_x, send_y, recv_y, send_f, recv_f, load_sem,
):
    nx, ny = lax.axis_size("gx"), lax.axis_size("gy")
    mx, my = lax.axis_index("gx"), lax.axis_index("gy")
    rows, cols = material.shape
    loads = [
        pltpu.make_async_copy(source, target, load_sem.at[i])
        for i, (source, target) in enumerate(
            (
                (material_in, material),
                (conduct_in, conduct),
                (joints_x_in, joints_x),
                (fields_in, fields),
                (joints_y_in, joints_y),
            )
        )
    ]
    for load in loads:
        load.start()

    barrier = pltpu.get_barrier_semaphore()
    peers_x = [far_first(mx, nx, k) for k in range(nx - 1)]
    peers_y = [lax.rem(my + k, ny) for k in range(1, ny)]
    for axis, peers in (("gx", peers_x), ("gy", peers_y)):
        for peer in peers:
            pl.semaphore_signal(
                barrier, inc=1, device_id={axis: peer}, device_id_type=pl.DeviceIdType.MESH
            )

    class Exchange:
        def __init__(self, axis, me, peers, held, slot, used, send, recv):
            self.axis, self.me, self.peers, self.held = axis, me, peers, held
            self.slot, self.used, self.send, self.recv = slot, used, send, recv
            self.slots = held.shape[0] // slot
            spare = self.slots - len(peers) - 1
            if spare > 0:
                held[(len(peers) + 1) * slot :, :] = jnp.ones(
                    (spare * slot, held.shape[1]), jnp.float32
                )

        def copy(self, k, owner):
            place = pl.multiple_of(owner * self.slot, self.slot)
            block = self.held.at[pl.ds(place, self.used), :]
            return pltpu.make_async_remote_copy(
                src_ref=block, dst_ref=block, send_sem=self.send.at[k],
                recv_sem=self.recv.at[owner], device_id={self.axis: self.peers[k]},
                device_id_type=pl.DeviceIdType.MESH,
            )

        def publish(self, lines):
            lines = list(lines) + [jnp.zeros_like(lines[0])] * (self.slot - len(lines))
            place = pl.multiple_of(self.me * self.slot, self.slot)
            self.held[pl.ds(place, self.slot), :] = jnp.concatenate(lines, axis=0)

        def start(self):
            for k in range(len(self.peers)):
                self.copy(k, self.me).start()

        def wait(self):
            for k, peer in enumerate(self.peers):
                self.copy(k, peer).wait_recv()

        def finish(self):
            for k in range(len(self.peers)):
                self.copy(k, self.me).wait_send()

        def item(self, q):
            return self.held[pl.ds(q, self.slots, stride=self.slot), :]

    ex_x = Exchange("gx", mx, peers_x, held_x, SLOT, ROWS, send_x, recv_x)
    ex_y = Exchange("gy", my, peers_y, held_y, SUB, SUB, send_y, recv_y)
    ex_f = Exchange("gy", my, peers_y, flow_y, SUB, 4, send_f, recv_f)

    def my_ends(comp, me, x0, x1):
        slots = x0.shape[0]
        base = 2 * comp * slots
        ends[pl.ds(base, slots), :] = x0
        ends[pl.ds(base + slots, slots), :] = x1
        return ends[pl.ds(me + base, 1), :], ends[pl.ds(me + base + slots, 1), :]

    for load in loads[:3]:
        load.wait()
    mat_t[...] = material[...].T
    jx = joints_x[...]
    span = cols // SUB
    along_x, mats = block_structure(conduct, mat_t, jx, mx * cols)
    loads[3].wait()
    for comp in range(2):
        field_t[comp] = fields[comp].T
    kept_x, lines = [], list(mats)
    for inner, shared in along_x:
        comp = len(kept_x)
        kept, f0, f1 = block_source(
            inner, [field_t[comp, pl.ds(t, SUB, stride=span), :] for t in range(span)]
        )
        kept_x.append(kept)
        lines += list(shared) + [f0, f1]
    ex_x.publish(lines)
    pl.semaphore_wait(barrier, nx + ny - 2)
    ex_x.start()

    loads[4].wait()
    jy = joints_y[...]
    span_y = rows // SUB
    along_y, mats = block_structure(conduct, material, jy, my * rows)
    ex_y.publish(list(mats) + list(along_y[0][1]) + list(along_y[1][1]))
    ex_y.start()

    ex_x.wait()
    mats = [ex_x.item(q) for q in range(2)]
    for comp in range(2):
        b, g0, g1, f0, f1 = [ex_x.item(2 + 5 * comp + q) for q in range(5)]
        structure = chain_structure(conduct, comp, (b, g0, g1), mats, jx, nx, cols)
        found = my_ends(comp, mx, *chain_source(structure, f0, f1))
        x = block_solve(along_x[comp][0], kept_x[comp], *found)
        for t in range(span):
            half_t[comp, pl.ds(t, SUB, stride=span), :] = x[t]
        half[comp] = half_t[comp].T

    kept_y, lines = [], []
    for comp in range(2):
        kept, f0, f1 = block_source(
            along_y[comp][0],
            [half[comp, pl.ds(t, SUB, stride=span_y), :] for t in range(span_y)],
        )
        kept_y.append(kept)
        lines += [f0, f1]
    ex_f.publish(lines)
    ex_f.start()
    ex_y.wait()
    mats = [ex_y.item(q) for q in range(2)]
    structures = [
        chain_structure(
            conduct, comp, [ex_y.item(2 + 3 * comp + q) for q in range(3)], mats, jy, ny, rows
        )
        for comp in range(2)
    ]
    ex_f.wait()
    for comp in range(2):
        f0, f1 = [ex_f.item(2 * comp + q) for q in range(2)]
        found = my_ends(comp, my, *chain_source(structures[comp], f0, f1))
        x = block_solve(along_y[comp][0], kept_y[comp], *found)
        for t in range(span_y):
            advanced[comp, pl.ds(t, SUB, stride=span_y), :] = x[t]
    ex_x.finish()
    ex_y.finish()
    ex_f.finish()


def write_out(half, advanced, half_out, advanced_out, sems):
    copies = [
        pltpu.make_async_copy(half, half_out, sems.at[0]),
        pltpu.make_async_copy(advanced, advanced_out, sems.at[1]),
    ]
    for copy in copies:
        copy.start()
    for copy in copies:
        copy.wait()


def per_device(nx, ny, fields, material, conduct, joints_x, joints_y):
    rows, cols = material.shape
    joints = joints_x.shape[1]
    vmem = pl.BlockSpec(memory_space=pltpu.VMEM)
    hbm = pl.BlockSpec(memory_space=pltpu.HBM)
    shape = jax.ShapeDtypeStruct(fields.shape, jnp.float32)
    sx, sy = max(nx, SUB), max(ny, SUB)
    solved = pl.pallas_call(
        kernel,
        out_shape=(shape, shape),
        in_specs=[hbm] * 5,
        out_specs=(vmem, vmem),
        scratch_shapes=[
            pltpu.VMEM((2, rows, cols), jnp.float32),
            pltpu.VMEM((rows, cols), jnp.int32),
            pltpu.SMEM(conduct.shape, jnp.float32),
            pltpu.VMEM((joints, rows), jnp.int32),
            pltpu.VMEM((joints, cols), jnp.int32),
            pltpu.VMEM((2, cols, rows), jnp.float32),
            pltpu.VMEM((cols, rows), jnp.int32),
            pltpu.VMEM((2, cols, rows), jnp.float32),
            pltpu.VMEM((sx * SLOT, rows), jnp.float32),
            pltpu.VMEM((sy * SUB, cols), jnp.float32),
            pltpu.VMEM((sy * SUB, cols), jnp.float32),
            pltpu.VMEM((4 * max(sx, sy), cols), jnp.float32),
            pltpu.SemaphoreType.DMA((nx,)),
            pltpu.SemaphoreType.DMA((nx,)),
            pltpu.SemaphoreType.DMA((ny,)),
            pltpu.SemaphoreType.DMA((ny,)),
            pltpu.SemaphoreType.DMA((ny,)),
            pltpu.SemaphoreType.DMA((ny,)),
            pltpu.SemaphoreType.DMA((5,)),
        ],
        compiler_params=pltpu.CompilerParams(
            collective_id=0, has_side_effects=True, vmem_limit_bytes=16 * 1024 * 1024
        ),
    )(
        *(
            pltpu.with_memory_space_constraint(x, pltpu.HBM)
            for x in (fields, material, conduct, joints_x.T, joints_y.T)
        )
    )
    return pl.pallas_call(
        write_out,
        out_shape=(shape, shape),
        in_specs=[vmem, vmem],
        out_specs=(hbm, hbm),
        scratch_shapes=[pltpu.SemaphoreType.DMA((2,))],
        compiler_params=pltpu.CompilerParams(vmem_limit_bytes=4 * 1024 * 1024),
    )(*solved)


def solution(mesh):
    return jax.shard_map(
        functools.partial(per_device, mesh.shape["gx"], mesh.shape["gy"]),
        mesh=mesh,
        in_specs=(P(None, "gy", "gx"), P("gy", "gx"), P(), P("gy", None), P("gx", None)),
        out_specs=(P(None, "gy", "gx"), P(None, "gy", "gx")),
        check_vma=False,
    )
```

```python
import functools

import jax
import jax.numpy as jnp
from jax import lax
from jax.experimental import pallas as pl
from jax.experimental.pallas import tpu as pltpu
from jax.sharding import PartitionSpec as P

MATERIALS = 8
FOURIER = 8192
DRYING = 4096
SCALES = (0.5 * FOURIER, 0.5 * DRYING)
SUB = 8
SLOT = 16
ROWS = 12


def inverse(x):
    guess = pl.reciprocal(x, approx=True)
    return guess * (2.0 - x * guess)


def lookup(conduct, comp, mats):
    low, mid, high = mats
    v = [conduct[comp, k] for k in range(MATERIALS)]
    pair = [jnp.where(low, v[2 * k + 1], v[2 * k]) for k in range(4)]
    quad = [jnp.where(mid, pair[2 * k + 1], pair[2 * k]) for k in range(2)]
    return jnp.where(high, quad[1], quad[0])


def bit_masks(mat):
    return (mat & 1) != 0, (mat & 2) != 0, (mat & 4) != 0


def fold(links, ground):
    ground = list(ground)
    index = list(range(len(ground)))
    plan = []
    while len(index) > 2:
        keep, merged = [index[0]], []
        p = 1
        while p < len(index):
            if p + 1 < len(index):
                a, k, b = index[p - 1 : p + 2]
                w = inverse(links[p - 1] + links[p] + ground[k])
                lo, hi = links[p - 1] * w, links[p] * w
                merged.append(links[p - 1] * hi)
                ground[a] = ground[a] + lo * ground[k]
                ground[b] = ground[b] + hi * ground[k]
                plan.append((a, k, b, lo, hi, w))
                keep.append(b)
                p += 2
            else:
                merged.append(links[p - 1])
                keep.append(index[p])
                p += 1
        index, links = keep, merged
    return plan, links[0], ground[0], ground[-1]


def fold_source(plan, source):
    source = list(source)
    for a, k, b, lo, hi, _ in plan:
        source[a] = source[a] + lo * source[k]
        source[b] = source[b] + hi * source[k]
    return source


def unfold(plan, source, first, last):
    x = {0: first, len(source) - 1: last}
    for a, k, b, lo, hi, w in reversed(plan):
        x[k] = source[k] * w + lo * x[a] + hi * x[b]
    return [x[k] for k in range(len(source))]


def roll(x, shift):
    return pltpu.roll(x, shift % x.shape[0], 0)


def block_structure(conduct, mat_ref, joints, base):
    span = mat_ref.shape[0] // SUB
    lane = mat_ref.shape[1]
    sub = lax.broadcasted_iota(jnp.int32, (SUB, lane), 0)
    bits = jnp.zeros((SUB, lane), jnp.int32)
    for k in range(joints.shape[0]):
        at = joints[k : k + 1, :] - base - sub * span
        bits = bits | jnp.where(
            (at >= 1) & (at <= span), jnp.left_shift(1, jnp.clip(at, 0, span)), 0
        )
    masks = []
    for t in range(span):
        last = mat_ref[pl.ds(t, SUB, stride=span), :]
        first = last if t == 0 else first
        masks.append(bit_masks(last))
    cut = [(bits & (1 << (t + 1))) != 0 for t in range(span)]
    out = []
    for comp in range(2):
        cond = [lookup(conduct, comp, m) for m in masks]
        after = cond[1:] + [roll(cond[0], -1)]
        face = [
            jnp.where(cut[t], 0.0, SCALES[comp] * (cond[t] + after[t])) for t in range(span)
        ]
        ones = jnp.ones((SUB, lane), jnp.float32)
        plan, b, gp, gq = fold(face[:-1], [ones] * span)
        link = jnp.where(sub == SUB - 1, 0.0, face[-1])
        wq = inverse(b + link + gq)
        lo = jnp.where(sub == SUB - 1, 0.0, b * wq)
        hi = link * wq
        c = jnp.where(sub == SUB - 1, b, b * hi)
        a = jnp.where(sub == 0, 0.0, roll(c, 1))
        g = gp + lo * gq + roll(hi * gq, 1)
        g_first = g
        steps = []
        s = 1
        while s < SUB:
            w = inverse(a + c + g)
            right = jnp.where((sub >= 1) & (sub <= SUB - 1 - s), c * w, 0.0)
            left = jnp.where(sub >= 1 + s, a * w, 0.0)
            steps.append((s, right, left))
            g_new = g + roll(right * g, s) + roll(left * g, -s)
            a_new = jnp.where(sub >= 1 + s, roll(right * a, s), a)
            c_new = jnp.where(sub <= SUB - 1 - s, roll(left * c, -s), c)
            a, c, g = a_new, c_new, g_new
            s *= 2
        w = inverse(a + c + g)
        aw, cw = a * w, c * w
        between = (aw * c)[1:2, :]
        ground0 = g_first[0:1, :] + (aw * g)[1:2, :]
        ground1 = (gq + cw * g)[SUB - 1 : SUB, :]
        inner = dict(
            plan=plan, b=b, link=link, wq=wq, lo=lo, hi=hi, steps=steps, w=w, aw=aw, cw=cw
        )
        out.append((inner, (between, ground0, ground1)))
    return out, (first[0:1, :].astype(jnp.float32), last[SUB - 1 : SUB, :].astype(jnp.float32))


def block_source(inner, source):
    source = fold_source(inner["plan"], source)
    fq = source[-1]
    f = source[0] + inner["lo"] * fq + roll(inner["hi"] * fq, 1)
    f_first = f
    for s, right, left in inner["steps"]:
        f = f + roll(right * f, s) + roll(left * f, -s)
    f0 = f_first[0:1, :] + (inner["aw"] * f)[1:2, :]
    f1 = (fq + inner["cw"] * f)[SUB - 1 : SUB, :]
    return (source, f), f0, f1


def block_solve(inner, kept, first, last):
    source, f = kept
    sub = lax.broadcasted_iota(jnp.int32, f.shape, 0)
    xp = f * inner["w"] + inner["aw"] * first + inner["cw"] * last
    xp = jnp.where(sub == 0, first, xp)
    xq = (source[-1] + inner["b"] * xp + inner["link"] * roll(xp, -1)) * inner["wq"]
    xq = jnp.where(sub == SUB - 1, last, xq)
    return unfold(inner["plan"], source, xp, xq)


def chain_structure(conduct, comp, rows, mats, joints, count, block):
    b, g0, g1 = rows
    slots = b.shape[0]
    pos = lax.broadcasted_iota(jnp.int32, b.shape, 0)
    cut = pos >= count - 1
    for k in range(joints.shape[0]):
        cut = cut | (joints[k : k + 1, :] == (pos + 1) * block)
    k0, k1 = [lookup(conduct, comp, bit_masks(m.astype(jnp.int32))) for m in mats]
    link = jnp.where(cut, 0.0, SCALES[comp] * (k1 + roll(k0, -1)))
    wr = inverse(b + link + g1)
    lo, hi = b * wr, link * wr
    c = b * hi
    a = roll(c, 1)
    g = g0 + lo * g1 + roll(hi * g1, 1)
    steps = []
    s = 1
    while s < count:
        w = inverse(a + c + g)
        right, left = c * w, a * w
        steps.append((s, right, left))
        g_new = g + roll(right * g, s) + roll(left * g, -s)
        a, c, g = roll(right * a, s), roll(left * c, -s), g_new
        s *= 2
    return b, link, wr, lo, hi, steps, inverse(g)


def chain_source(structure, f0, f1):
    b, link, wr, lo, hi, steps, w = structure
    f = f0 + lo * f1 + roll(hi * f1, 1)
    for s, right, left in steps:
        f = f + roll(right * f, s) + roll(left * f, -s)
    x0 = f * w
    x1 = (f1 + b * x0 + link * roll(x0, -1)) * wr
    return x0, x1


def over(value, n):
    if n & (n - 1):
        return lax.div(value, n)
    return lax.shift_right_arithmetic(value, n.bit_length() - 1)


def far_first(me, n, k):
    down = n - 1 - k - over(me + k + 1, n)
    up = k + over(k - me + n, n)
    half = over(2 * me, n)
    return half * up + (1 - half) * down


def kernel(
    fields_in, material_in, conduct_in, joints_x_in, joints_y_in, half, advanced,
    fields, material, conduct, joints_x, joints_y,
    field_t, mat_t, half_t, held_x, held_y, flow_y, ends,
    send_x, recv_x, send_y, recv_y, send_f, recv_f, load_sem,
):
    nx, ny = lax.axis_size("gx"), lax.axis_size("gy")
    mx, my = lax.axis_index("gx"), lax.axis_index("gy")
    rows, cols = material.shape
    loads = [
        pltpu.make_async_copy(source, target, load_sem.at[i])
        for i, (source, target) in enumerate(
            (
                (material_in, material),
                (conduct_in, conduct),
                (joints_x_in, joints_x),
                (fields_in, fields),
                (joints_y_in, joints_y),
            )
        )
    ]
    for load in loads:
        load.start()

    barrier = pltpu.get_barrier_semaphore()
    peers_x = [far_first(mx, nx, k) for k in range(nx - 1)]
    peers_y = [my + k - ny * over(my + k, ny) for k in range(1, ny)]
    for axis, peers in (("gx", peers_x), ("gy", peers_y)):
        for peer in peers:
            pl.semaphore_signal(
                barrier, inc=1, device_id={axis: peer}, device_id_type=pl.DeviceIdType.MESH
            )

    class Exchange:
        def __init__(self, axis, me, peers, held, slot, used, send, recv):
            self.axis, self.me, self.peers, self.held = axis, me, peers, held
            self.slot, self.used, self.send, self.recv = slot, used, send, recv
            self.slots = held.shape[0] // slot
            spare = self.slots - len(peers) - 1
            if spare > 0:
                held[(len(peers) + 1) * slot :, :] = jnp.ones(
                    (spare * slot, held.shape[1]), jnp.float32
                )

        def copy(self, k, owner):
            place = pl.multiple_of(owner * self.slot, self.slot)
            block = self.held.at[pl.ds(place, self.used), :]
            return pltpu.make_async_remote_copy(
                src_ref=block, dst_ref=block, send_sem=self.send.at[k],
                recv_sem=self.recv.at[owner], device_id={self.axis: self.peers[k]},
                device_id_type=pl.DeviceIdType.MESH,
            )

        def publish(self, lines):
            lines = list(lines) + [jnp.zeros_like(lines[0])] * (self.slot - len(lines))
            place = pl.multiple_of(self.me * self.slot, self.slot)
            self.held[pl.ds(place, self.slot), :] = jnp.concatenate(lines, axis=0)

        def start(self):
            for k in range(len(self.peers)):
                self.copy(k, self.me).start()

        def wait(self):
            for k, peer in enumerate(self.peers):
                self.copy(k, peer).wait_recv()

        def finish(self):
            for k in range(len(self.peers)):
                self.copy(k, self.me).wait_send()

        def item(self, q):
            return self.held[pl.ds(q, self.slots, stride=self.slot), :]

    ex_x = Exchange("gx", mx, peers_x, held_x, SLOT, ROWS, send_x, recv_x)
    ex_y = Exchange("gy", my, peers_y, held_y, SUB, SUB, send_y, recv_y)
    ex_f = Exchange("gy", my, peers_y, flow_y, SUB, 4, send_f, recv_f)

    def my_ends(comp, me, x0, x1):
        slots = x0.shape[0]
        base = 2 * comp * slots
        ends[pl.ds(base, slots), :] = x0
        ends[pl.ds(base + slots, slots), :] = x1
        return ends[pl.ds(me + base, 1), :], ends[pl.ds(me + base + slots, 1), :]

    for load in loads[:3]:
        load.wait()
    mat_t[...] = material[...].T
    jx = joints_x[...]
    span = cols // SUB
    along_x, mats = block_structure(conduct, mat_t, jx, mx * cols)
    loads[3].wait()
    for comp in range(2):
        field_t[comp] = fields[comp].T
    kept_x, lines = [], list(mats)
    for inner, shared in along_x:
        comp = len(kept_x)
        kept, f0, f1 = block_source(
            inner, [field_t[comp, pl.ds(t, SUB, stride=span), :] for t in range(span)]
        )
        kept_x.append(kept)
        lines += list(shared) + [f0, f1]
    ex_x.publish(lines)
    pl.semaphore_wait(barrier, nx + ny - 2)
    ex_x.start()

    loads[4].wait()
    jy = joints_y[...]
    span_y = rows // SUB
    along_y, mats = block_structure(conduct, material, jy, my * rows)
    ex_y.publish(list(mats) + list(along_y[0][1]) + list(along_y[1][1]))
    ex_y.start()

    ex_x.wait()
    mats = [ex_x.item(q) for q in range(2)]
    for comp in range(2):
        b, g0, g1, f0, f1 = [ex_x.item(2 + 5 * comp + q) for q in range(5)]
        structure = chain_structure(conduct, comp, (b, g0, g1), mats, jx, nx, cols)
        found = my_ends(comp, mx, *chain_source(structure, f0, f1))
        x = block_solve(along_x[comp][0], kept_x[comp], *found)
        for t in range(span):
            half_t[comp, pl.ds(t, SUB, stride=span), :] = x[t]
        half[comp] = half_t[comp].T

    kept_y, lines = [], []
    for comp in range(2):
        kept, f0, f1 = block_source(
            along_y[comp][0],
            [half[comp, pl.ds(t, SUB, stride=span_y), :] for t in range(span_y)],
        )
        kept_y.append(kept)
        lines += [f0, f1]
    ex_f.publish(lines)
    ex_f.start()
    ex_y.wait()
    mats = [ex_y.item(q) for q in range(2)]
    structures = [
        chain_structure(
            conduct, comp, [ex_y.item(2 + 3 * comp + q) for q in range(3)], mats, jy, ny, rows
        )
        for comp in range(2)
    ]
    ex_f.wait()
    for comp in range(2):
        f0, f1 = [ex_f.item(2 * comp + q) for q in range(2)]
        found = my_ends(comp, my, *chain_source(structures[comp], f0, f1))
        x = block_solve(along_y[comp][0], kept_y[comp], *found)
        for t in range(span_y):
            advanced[comp, pl.ds(t, SUB, stride=span_y), :] = x[t]
    ex_x.finish()
    ex_y.finish()
    ex_f.finish()


def write_out(half, advanced, half_out, advanced_out, sems):
    copies = [
        pltpu.make_async_copy(half, half_out, sems.at[0]),
        pltpu.make_async_copy(advanced, advanced_out, sems.at[1]),
    ]
    for copy in copies:
        copy.start()
    for copy in copies:
        copy.wait()


def per_device(nx, ny, fields, material, conduct, joints_x, joints_y):
    rows, cols = material.shape
    joints = joints_x.shape[1]
    vmem = pl.BlockSpec(memory_space=pltpu.VMEM)
    hbm = pl.BlockSpec(memory_space=pltpu.HBM)
    shape = jax.ShapeDtypeStruct(fields.shape, jnp.float32)
    sx, sy = max(nx, SUB), max(ny, SUB)
    solved = pl.pallas_call(
        kernel,
        out_shape=(shape, shape),
        in_specs=[hbm] * 5,
        out_specs=(vmem, vmem),
        scratch_shapes=[
            pltpu.VMEM((2, rows, cols), jnp.float32),
            pltpu.VMEM((rows, cols), jnp.int32),
            pltpu.SMEM(conduct.shape, jnp.float32),
            pltpu.VMEM((joints, rows), jnp.int32),
            pltpu.VMEM((joints, cols), jnp.int32),
            pltpu.VMEM((2, cols, rows), jnp.float32),
            pltpu.VMEM((cols, rows), jnp.int32),
            pltpu.VMEM((2, cols, rows), jnp.float32),
            pltpu.VMEM((sx * SLOT, rows), jnp.float32),
            pltpu.VMEM((sy * SUB, cols), jnp.float32),
            pltpu.VMEM((sy * SUB, cols), jnp.float32),
            pltpu.VMEM((4 * max(sx, sy), cols), jnp.float32),
            pltpu.SemaphoreType.DMA((nx,)),
            pltpu.SemaphoreType.DMA((nx,)),
            pltpu.SemaphoreType.DMA((ny,)),
            pltpu.SemaphoreType.DMA((ny,)),
            pltpu.SemaphoreType.DMA((ny,)),
            pltpu.SemaphoreType.DMA((ny,)),
            pltpu.SemaphoreType.DMA((5,)),
        ],
        compiler_params=pltpu.CompilerParams(
            collective_id=0, has_side_effects=True, vmem_limit_bytes=16 * 1024 * 1024
        ),
    )(
        *(
            pltpu.with_memory_space_constraint(x, pltpu.HBM)
            for x in (fields, material, conduct, joints_x.T, joints_y.T)
        )
    )
    return pl.pallas_call(
        write_out,
        out_shape=(shape, shape),
        in_specs=[vmem, vmem],
        out_specs=(hbm, hbm),
        scratch_shapes=[pltpu.SemaphoreType.DMA((2,))],
        compiler_params=pltpu.CompilerParams(vmem_limit_bytes=4 * 1024 * 1024),
    )(*solved)


def solution(mesh):
    return jax.shard_map(
        functools.partial(per_device, mesh.shape["gx"], mesh.shape["gy"]),
        mesh=mesh,
        in_specs=(P(None, "gy", "gx"), P("gy", "gx"), P(), P("gy", None), P("gx", None)),
        out_specs=(P(None, "gy", "gx"), P(None, "gy", "gx")),
        check_vma=False,
    )
```

```python
import functools

import jax
import jax.numpy as jnp
from jax import lax
from jax.experimental import pallas as pl
from jax.experimental.pallas import tpu as pltpu
from jax.sharding import PartitionSpec as P

MATERIALS = 8
FOURIER = 8192
DRYING = 4096
SCALES = (0.5 * FOURIER, 0.5 * DRYING)
SUB = 8
SLOT = 16
ROWS = 12


def inverse(x):
    guess = pl.reciprocal(x, approx=True)
    return guess * (2.0 - x * guess)


def lookup(conduct, comp, mats):
    low, mid, high = mats
    v = [conduct[comp, k] for k in range(MATERIALS)]
    pair = [jnp.where(low, v[2 * k + 1], v[2 * k]) for k in range(4)]
    quad = [jnp.where(mid, pair[2 * k + 1], pair[2 * k]) for k in range(2)]
    return jnp.where(high, quad[1], quad[0])


def bit_masks(mat):
    return (mat & 1) != 0, (mat & 2) != 0, (mat & 4) != 0


def fold(links, ground):
    ground = list(ground)
    index = list(range(len(ground)))
    plan = []
    while len(index) > 2:
        keep, merged = [index[0]], []
        p = 1
        while p < len(index):
            if p + 1 < len(index):
                a, k, b = index[p - 1 : p + 2]
                w = inverse(links[p - 1] + links[p] + ground[k])
                lo, hi = links[p - 1] * w, links[p] * w
                merged.append(links[p - 1] * hi)
                ground[a] = ground[a] + lo * ground[k]
                ground[b] = ground[b] + hi * ground[k]
                plan.append((a, k, b, lo, hi, w))
                keep.append(b)
                p += 2
            else:
                merged.append(links[p - 1])
                keep.append(index[p])
                p += 1
        index, links = keep, merged
    return plan, links[0], ground[0], ground[-1]


def fold_source(plan, source):
    source = list(source)
    for a, k, b, lo, hi, _ in plan:
        source[a] = source[a] + lo * source[k]
        source[b] = source[b] + hi * source[k]
    return source


def unfold(plan, source, first, last):
    x = {0: first, len(source) - 1: last}
    for a, k, b, lo, hi, w in reversed(plan):
        x[k] = source[k] * w + lo * x[a] + hi * x[b]
    return [x[k] for k in range(len(source))]


def roll(x, shift):
    return pltpu.roll(x, shift % x.shape[0], 0)


def block_structure(conduct, mat_ref, joints, base):
    span = mat_ref.shape[0] // SUB
    lane = mat_ref.shape[1]
    sub = lax.broadcasted_iota(jnp.int32, (SUB, lane), 0)
    bits = jnp.zeros((SUB, lane), jnp.int32)
    for k in range(joints.shape[0]):
        at = joints[k : k + 1, :] - base - sub * span
        bits = bits | jnp.where(
            (at >= 1) & (at <= span), jnp.left_shift(1, jnp.clip(at, 0, span)), 0
        )
    masks = []
    for t in range(span):
        last = mat_ref[pl.ds(t, SUB, stride=span), :]
        first = last if t == 0 else first
        masks.append(bit_masks(last))
    cut = [(bits & (1 << (t + 1))) != 0 for t in range(span)]
    out = []
    for comp in range(2):
        cond = [lookup(conduct, comp, m) for m in masks]
        after = cond[1:] + [roll(cond[0], -1)]
        face = [
            jnp.where(cut[t], 0.0, SCALES[comp] * (cond[t] + after[t])) for t in range(span)
        ]
        ones = jnp.ones((SUB, lane), jnp.float32)
        plan, b, gp, gq = fold(face[:-1], [ones] * span)
        link = jnp.where(sub == SUB - 1, 0.0, face[-1])
        wq = inverse(b + link + gq)
        lo = jnp.where(sub == SUB - 1, 0.0, b * wq)
        hi = link * wq
        c = jnp.where(sub == SUB - 1, b, b * hi)
        a = jnp.where(sub == 0, 0.0, roll(c, 1))
        g = gp + lo * gq + roll(hi * gq, 1)
        g_first = g
        steps = []
        s = 1
        while s < SUB:
            w = inverse(a + c + g)
            right = jnp.where((sub >= 1) & (sub <= SUB - 1 - s), c * w, 0.0)
            left = jnp.where(sub >= 1 + s, a * w, 0.0)
            steps.append((s, right, left))
            g_new = g + roll(right * g, s) + roll(left * g, -s)
            a_new = jnp.where(sub >= 1 + s, roll(right * a, s), a)
            c_new = jnp.where(sub <= SUB - 1 - s, roll(left * c, -s), c)
            a, c, g = a_new, c_new, g_new
            s *= 2
        w = inverse(a + c + g)
        aw, cw = a * w, c * w
        between = (aw * c)[1:2, :]
        ground0 = g_first[0:1, :] + (aw * g)[1:2, :]
        ground1 = (gq + cw * g)[SUB - 1 : SUB, :]
        inner = dict(
            plan=plan, b=b, link=link, wq=wq, lo=lo, hi=hi, steps=steps, w=w, aw=aw, cw=cw
        )
        out.append((inner, (between, ground0, ground1)))
    return out, (first[0:1, :].astype(jnp.float32), last[SUB - 1 : SUB, :].astype(jnp.float32))


def block_source(inner, source):
    source = fold_source(inner["plan"], source)
    fq = source[-1]
    f = source[0] + inner["lo"] * fq + roll(inner["hi"] * fq, 1)
    f_first = f
    for s, right, left in inner["steps"]:
        f = f + roll(right * f, s) + roll(left * f, -s)
    f0 = f_first[0:1, :] + (inner["aw"] * f)[1:2, :]
    f1 = (fq + inner["cw"] * f)[SUB - 1 : SUB, :]
    return (source, f), f0, f1


def block_solve(inner, kept, first, last):
    source, f = kept
    sub = lax.broadcasted_iota(jnp.int32, f.shape, 0)
    xp = f * inner["w"] + inner["aw"] * first + inner["cw"] * last
    xp = jnp.where(sub == 0, first, xp)
    xq = (source[-1] + inner["b"] * xp + inner["link"] * roll(xp, -1)) * inner["wq"]
    xq = jnp.where(sub == SUB - 1, last, xq)
    return unfold(inner["plan"], source, xp, xq)


def chain_structure(conduct, comp, rows, mats, joints, count, block):
    b, g0, g1 = rows
    slots = b.shape[0]
    pos = lax.broadcasted_iota(jnp.int32, b.shape, 0)
    cut = pos >= count - 1
    for k in range(joints.shape[0]):
        cut = cut | (joints[k : k + 1, :] == (pos + 1) * block)
    k0, k1 = [lookup(conduct, comp, bit_masks(m.astype(jnp.int32))) for m in mats]
    link = jnp.where(cut, 0.0, SCALES[comp] * (k1 + roll(k0, -1)))
    wr = inverse(b + link + g1)
    lo, hi = b * wr, link * wr
    c = b * hi
    a = roll(c, 1)
    g = g0 + lo * g1 + roll(hi * g1, 1)
    steps = []
    s = 1
    while s < count:
        w = inverse(a + c + g)
        right, left = c * w, a * w
        steps.append((s, right, left))
        g_new = g + roll(right * g, s) + roll(left * g, -s)
        a, c, g = roll(right * a, s), roll(left * c, -s), g_new
        s *= 2
    return b, link, wr, lo, hi, steps, inverse(g)


def chain_source(structure, f0, f1):
    b, link, wr, lo, hi, steps, w = structure
    f = f0 + lo * f1 + roll(hi * f1, 1)
    for s, right, left in steps:
        f = f + roll(right * f, s) + roll(left * f, -s)
    x0 = f * w
    x1 = (f1 + b * x0 + link * roll(x0, -1)) * wr
    return x0, x1


def over(value, n):
    if n & (n - 1):
        return lax.div(value, n)
    return lax.shift_right_arithmetic(value, n.bit_length() - 1)


def far_first(me, n, k):
    down = n - 1 - k - over(me + k + 1, n)
    up = k + over(k - me + n, n)
    half = over(2 * me, n)
    return half * up + (1 - half) * down


def kernel(
    fields_in, material_in, conduct_in, joints_x_in, joints_y_in, half, advanced,
    fields, material, conduct, joints_x, joints_y,
    field_t, mat_t, half_t, resp_x, resp_y, part_y, mix, held_x, held_y, flow_y, ends,
    send_x, recv_x, send_y, recv_y, send_f, recv_f, load_sem,
):
    nx, ny = lax.axis_size("gx"), lax.axis_size("gy")
    mx, my = lax.axis_index("gx"), lax.axis_index("gy")
    rows, cols = material.shape
    loads = [
        pltpu.make_async_copy(source, target, load_sem.at[i])
        for i, (source, target) in enumerate(
            (
                (material_in, material),
                (conduct_in, conduct),
                (joints_x_in, joints_x),
                (fields_in, fields),
                (joints_y_in, joints_y),
            )
        )
    ]
    for load in loads:
        load.start()

    barrier = pltpu.get_barrier_semaphore()
    peers_x = [far_first(mx, nx, k) for k in range(nx - 1)]
    peers_y = [my + k - ny * over(my + k, ny) for k in range(1, ny)]
    for axis, peers in (("gx", peers_x), ("gy", peers_y)):
        for peer in peers:
            pl.semaphore_signal(
                barrier, inc=1, device_id={axis: peer}, device_id_type=pl.DeviceIdType.MESH
            )

    class Exchange:
        def __init__(self, axis, me, peers, held, slot, used, send, recv):
            self.axis, self.me, self.peers, self.held = axis, me, peers, held
            self.slot, self.used, self.send, self.recv = slot, used, send, recv
            self.slots = held.shape[0] // slot
            spare = self.slots - len(peers) - 1
            if spare > 0:
                held[(len(peers) + 1) * slot :, :] = jnp.ones(
                    (spare * slot, held.shape[1]), jnp.float32
                )

        def copy(self, k, owner):
            place = pl.multiple_of(owner * self.slot, self.slot)
            block = self.held.at[pl.ds(place, self.used), :]
            return pltpu.make_async_remote_copy(
                src_ref=block, dst_ref=block, send_sem=self.send.at[k],
                recv_sem=self.recv.at[owner], device_id={self.axis: self.peers[k]},
                device_id_type=pl.DeviceIdType.MESH,
            )

        def publish(self, lines):
            lines = list(lines) + [jnp.zeros_like(lines[0])] * (self.slot - len(lines))
            place = pl.multiple_of(self.me * self.slot, self.slot)
            self.held[pl.ds(place, self.slot), :] = jnp.concatenate(lines, axis=0)

        def start(self):
            for k in range(len(self.peers)):
                self.copy(k, self.me).start()

        def wait(self):
            for k, peer in enumerate(self.peers):
                self.copy(k, peer).wait_recv()

        def finish(self):
            for k in range(len(self.peers)):
                self.copy(k, self.me).wait_send()

        def item(self, q):
            return self.held[pl.ds(q, self.slots, stride=self.slot), :]

    ex_x = Exchange("gx", mx, peers_x, held_x, SLOT, ROWS, send_x, recv_x)
    ex_y = Exchange("gy", my, peers_y, held_y, SUB, SUB, send_y, recv_y)
    ex_f = Exchange("gy", my, peers_y, flow_y, SUB, 4, send_f, recv_f)

    def my_ends(comp, me, x0, x1):
        slots = x0.shape[0]
        base = 2 * comp * slots
        ends[pl.ds(base, slots), :] = x0
        ends[pl.ds(base + slots, slots), :] = x1
        return ends[pl.ds(me + base, 1), :], ends[pl.ds(me + base + slots, 1), :]

    for load in loads[:3]:
        load.wait()
    mat_t[...] = material[...].T
    jx = joints_x[...]
    span = cols // SUB
    along_x, mats = block_structure(conduct, mat_t, jx, mx * cols)
    loads[3].wait()
    for comp in range(2):
        field_t[comp] = fields[comp].T
    kept_x, lines = [], list(mats)
    for inner, shared in along_x:
        comp = len(kept_x)
        kept, f0, f1 = block_source(
            inner, [field_t[comp, pl.ds(t, SUB, stride=span), :] for t in range(span)]
        )
        kept_x.append(kept)
        lines += list(shared) + [f0, f1]
    ex_x.publish(lines)
    pl.semaphore_wait(barrier, nx + ny - 2)
    ex_x.start()

    loads[4].wait()
    jy = joints_y[...]
    span_y = rows // SUB
    along_y, mats = block_structure(conduct, material, jy, my * rows)
    ex_y.publish(list(mats) + list(along_y[0][1]) + list(along_y[1][1]))
    ex_y.start()

    zero = jnp.zeros((SUB, cols), jnp.float32)
    one = jnp.ones((SUB, cols), jnp.float32)
    none_x, none_y = ([zero] * span, zero), ([zero] * span_y, zero)

    def keep(ref, index, values):
        for t, value in enumerate(values):
            ref[index, pl.ds(t, SUB, stride=len(values)), :] = value

    for comp in range(2):
        inner = along_x[comp][0]
        for q, values in enumerate(
            (
                block_solve(inner, kept_x[comp], zero, zero),
                block_solve(inner, none_x, one, zero),
                block_solve(inner, none_x, zero, one),
            )
        ):
            keep(resp_x, 3 * comp + q, values)
        inner = along_y[comp][0]
        for q, values in enumerate(
            (block_solve(inner, none_y, one, zero), block_solve(inner, none_y, zero, one))
        ):
            keep(resp_y, 2 * comp + q, values)
    base = []
    for comp in range(2):
        turned = [resp_x[3 * comp + q].T for q in range(3)]
        for q in range(2):
            weight = resp_y[2 * comp + q]
            base.append(jnp.sum(weight * turned[0], axis=0, keepdims=True))
            for p in range(2):
                mix[comp, p * rows : (p + 1) * rows, q * cols : (q + 1) * cols] = (
                    weight * turned[1 + p]
                )

    ex_x.wait()
    mats = [ex_x.item(q) for q in range(2)]
    found_x, lines = [], []
    for comp in range(2):
        b, g0, g1, f0, f1 = [ex_x.item(2 + 5 * comp + q) for q in range(5)]
        structure = chain_structure(conduct, comp, (b, g0, g1), mats, jx, nx, cols)
        found = my_ends(comp, mx, *chain_source(structure, f0, f1))
        found_x.append(found)
        sides = jnp.broadcast_to(jnp.concatenate(found, axis=1), (SUB, 2 * rows))
        flow = jnp.dot(
            sides, mix[comp], precision=lax.Precision.HIGHEST,
            preferred_element_type=jnp.float32,
        )
        for q in range(2):
            lines.append(base[2 * comp + q] + flow[0:1, q * cols : (q + 1) * cols])
    ex_f.publish(lines)
    ex_f.start()

    for comp in range(2):
        first, last = found_x[comp]
        half_t[comp] = (
            resp_x[3 * comp] + resp_x[3 * comp + 1] * first + resp_x[3 * comp + 2] * last
        )
        half[comp] = half_t[comp].T
        inner = along_y[comp][0]
        kept, _, _ = block_source(
            inner, [half[comp, pl.ds(t, SUB, stride=span_y), :] for t in range(span_y)]
        )
        keep(part_y, comp, block_solve(inner, kept, zero, zero))
    ex_y.wait()
    mats = [ex_y.item(q) for q in range(2)]
    structures = [
        chain_structure(
            conduct, comp, [ex_y.item(2 + 3 * comp + q) for q in range(3)], mats, jy, ny, rows
        )
        for comp in range(2)
    ]
    ex_f.wait()
    for comp in range(2):
        f0, f1 = [ex_f.item(2 * comp + q) for q in range(2)]
        first, last = my_ends(comp, my, *chain_source(structures[comp], f0, f1))
        advanced[comp] = (
            part_y[comp] + resp_y[2 * comp] * first + resp_y[2 * comp + 1] * last
        )
    ex_x.finish()
    ex_y.finish()
    ex_f.finish()


def write_out(half, advanced, half_out, advanced_out, sems):
    copies = [
        pltpu.make_async_copy(half, half_out, sems.at[0]),
        pltpu.make_async_copy(advanced, advanced_out, sems.at[1]),
    ]
    for copy in copies:
        copy.start()
    for copy in copies:
        copy.wait()


def per_device(nx, ny, fields, material, conduct, joints_x, joints_y):
    rows, cols = material.shape
    joints = joints_x.shape[1]
    vmem = pl.BlockSpec(memory_space=pltpu.VMEM)
    hbm = pl.BlockSpec(memory_space=pltpu.HBM)
    shape = jax.ShapeDtypeStruct(fields.shape, jnp.float32)
    sx, sy = max(nx, SUB), max(ny, SUB)
    solved = pl.pallas_call(
        kernel,
        out_shape=(shape, shape),
        in_specs=[hbm] * 5,
        out_specs=(vmem, vmem),
        scratch_shapes=[
            pltpu.VMEM((2, rows, cols), jnp.float32),
            pltpu.VMEM((rows, cols), jnp.int32),
            pltpu.SMEM(conduct.shape, jnp.float32),
            pltpu.VMEM((joints, rows), jnp.int32),
            pltpu.VMEM((joints, cols), jnp.int32),
            pltpu.VMEM((2, cols, rows), jnp.float32),
            pltpu.VMEM((cols, rows), jnp.int32),
            pltpu.VMEM((2, cols, rows), jnp.float32),
            pltpu.VMEM((6, cols, rows), jnp.float32),
            pltpu.VMEM((4, rows, cols), jnp.float32),
            pltpu.VMEM((2, rows, cols), jnp.float32),
            pltpu.VMEM((2, 2 * rows, 2 * cols), jnp.float32),
            pltpu.VMEM((sx * SLOT, rows), jnp.float32),
            pltpu.VMEM((sy * SUB, cols), jnp.float32),
            pltpu.VMEM((sy * SUB, cols), jnp.float32),
            pltpu.VMEM((4 * max(sx, sy), cols), jnp.float32),
            pltpu.SemaphoreType.DMA((nx,)),
            pltpu.SemaphoreType.DMA((nx,)),
            pltpu.SemaphoreType.DMA((ny,)),
            pltpu.SemaphoreType.DMA((ny,)),
            pltpu.SemaphoreType.DMA((ny,)),
            pltpu.SemaphoreType.DMA((ny,)),
            pltpu.SemaphoreType.DMA((5,)),
        ],
        compiler_params=pltpu.CompilerParams(
            collective_id=0, has_side_effects=True, vmem_limit_bytes=16 * 1024 * 1024
        ),
    )(
        *(
            pltpu.with_memory_space_constraint(x, pltpu.HBM)
            for x in (fields, material, conduct, joints_x.T, joints_y.T)
        )
    )
    return pl.pallas_call(
        write_out,
        out_shape=(shape, shape),
        in_specs=[vmem, vmem],
        out_specs=(hbm, hbm),
        scratch_shapes=[pltpu.SemaphoreType.DMA((2,))],
        compiler_params=pltpu.CompilerParams(vmem_limit_bytes=4 * 1024 * 1024),
    )(*solved)


def solution(mesh):
    return jax.shard_map(
        functools.partial(per_device, mesh.shape["gx"], mesh.shape["gy"]),
        mesh=mesh,
        in_specs=(P(None, "gy", "gx"), P("gy", "gx"), P(), P("gy", None), P("gx", None)),
        out_specs=(P(None, "gy", "gx"), P(None, "gy", "gx")),
        check_vma=False,
    )
```

```python
import functools

import jax
import jax.numpy as jnp
from jax import lax
from jax.experimental import pallas as pl
from jax.experimental.pallas import tpu as pltpu
from jax.sharding import PartitionSpec as P

MATERIALS = 8
FOURIER = 8192
DRYING = 4096
SCALES = (0.5 * FOURIER, 0.5 * DRYING)
SUB = 8
SLOT = 16
ROWS = 12


def inverse(x):
    guess = pl.reciprocal(x, approx=True)
    return guess * (2.0 - x * guess)


def lookup(conduct, comp, mats):
    low, mid, high = mats
    v = [conduct[comp, k] for k in range(MATERIALS)]
    pair = [jnp.where(low, v[2 * k + 1], v[2 * k]) for k in range(4)]
    quad = [jnp.where(mid, pair[2 * k + 1], pair[2 * k]) for k in range(2)]
    return jnp.where(high, quad[1], quad[0])


def bit_masks(mat):
    return (mat & 1) != 0, (mat & 2) != 0, (mat & 4) != 0


def fold(links, ground):
    ground = list(ground)
    index = list(range(len(ground)))
    plan = []
    while len(index) > 2:
        keep, merged = [index[0]], []
        p = 1
        while p < len(index):
            if p + 1 < len(index):
                a, k, b = index[p - 1 : p + 2]
                w = inverse(links[p - 1] + links[p] + ground[k])
                lo, hi = links[p - 1] * w, links[p] * w
                merged.append(links[p - 1] * hi)
                ground[a] = ground[a] + lo * ground[k]
                ground[b] = ground[b] + hi * ground[k]
                plan.append((a, k, b, lo, hi, w))
                keep.append(b)
                p += 2
            else:
                merged.append(links[p - 1])
                keep.append(index[p])
                p += 1
        index, links = keep, merged
    return plan, links[0], ground[0], ground[-1]


def fold_source(plan, source):
    source = list(source)
    for a, k, b, lo, hi, _ in plan:
        source[a] = source[a] + lo * source[k]
        source[b] = source[b] + hi * source[k]
    return source


def unfold(plan, source, first, last):
    x = {0: first, len(source) - 1: last}
    for a, k, b, lo, hi, w in reversed(plan):
        x[k] = source[k] * w + lo * x[a] + hi * x[b]
    return [x[k] for k in range(len(source))]


def roll(x, shift):
    return pltpu.roll(x, shift % x.shape[0], 0)


def block_structure(conduct, mat_ref, joints, base):
    span = mat_ref.shape[0] // SUB
    lane = mat_ref.shape[1]
    sub = lax.broadcasted_iota(jnp.int32, (SUB, lane), 0)
    bits = jnp.zeros((SUB, lane), jnp.int32)
    for k in range(joints.shape[0]):
        at = joints[k : k + 1, :] - base - sub * span
        bits = bits | jnp.where(
            (at >= 1) & (at <= span), jnp.left_shift(1, jnp.clip(at, 0, span)), 0
        )
    masks = []
    for t in range(span):
        last = mat_ref[pl.ds(t, SUB, stride=span), :]
        first = last if t == 0 else first
        masks.append(bit_masks(last))
    cut = [(bits & (1 << (t + 1))) != 0 for t in range(span)]
    out = []
    for comp in range(2):
        cond = [lookup(conduct, comp, m) for m in masks]
        after = cond[1:] + [roll(cond[0], -1)]
        face = [
            jnp.where(cut[t], 0.0, SCALES[comp] * (cond[t] + after[t])) for t in range(span)
        ]
        ones = jnp.ones((SUB, lane), jnp.float32)
        plan, b, gp, gq = fold(face[:-1], [ones] * span)
        link = jnp.where(sub == SUB - 1, 0.0, face[-1])
        wq = inverse(b + link + gq)
        lo = jnp.where(sub == SUB - 1, 0.0, b * wq)
        hi = link * wq
        c = jnp.where(sub == SUB - 1, b, b * hi)
        a = jnp.where(sub == 0, 0.0, roll(c, 1))
        g = gp + lo * gq + roll(hi * gq, 1)
        g_first = g
        steps = []
        s = 1
        while s < SUB:
            w = inverse(a + c + g)
            right = jnp.where((sub >= 1) & (sub <= SUB - 1 - s), c * w, 0.0)
            left = jnp.where(sub >= 1 + s, a * w, 0.0)
            steps.append((s, right, left))
            g_new = g + roll(right * g, s) + roll(left * g, -s)
            a_new = jnp.where(sub >= 1 + s, roll(right * a, s), a)
            c_new = jnp.where(sub <= SUB - 1 - s, roll(left * c, -s), c)
            a, c, g = a_new, c_new, g_new
            s *= 2
        w = inverse(a + c + g)
        aw, cw = a * w, c * w
        between = (aw * c)[1:2, :]
        ground0 = g_first[0:1, :] + (aw * g)[1:2, :]
        ground1 = (gq + cw * g)[SUB - 1 : SUB, :]
        inner = dict(
            plan=plan, b=b, link=link, wq=wq, lo=lo, hi=hi, steps=steps, w=w, aw=aw, cw=cw
        )
        out.append((inner, (between, ground0, ground1)))
    return out, (first[0:1, :].astype(jnp.float32), last[SUB - 1 : SUB, :].astype(jnp.float32))


def block_source(inner, source):
    source = fold_source(inner["plan"], source)
    fq = source[-1]
    f = source[0] + inner["lo"] * fq + roll(inner["hi"] * fq, 1)
    f_first = f
    for s, right, left in inner["steps"]:
        f = f + roll(right * f, s) + roll(left * f, -s)
    f0 = f_first[0:1, :] + (inner["aw"] * f)[1:2, :]
    f1 = (fq + inner["cw"] * f)[SUB - 1 : SUB, :]
    return (source, f), f0, f1


def block_solve(inner, kept, first, last):
    source, f = kept
    sub = lax.broadcasted_iota(jnp.int32, f.shape, 0)
    xp = f * inner["w"] + inner["aw"] * first + inner["cw"] * last
    xp = jnp.where(sub == 0, first, xp)
    xq = (source[-1] + inner["b"] * xp + inner["link"] * roll(xp, -1)) * inner["wq"]
    xq = jnp.where(sub == SUB - 1, last, xq)
    return unfold(inner["plan"], source, xp, xq)


def chain_structure(conduct, comp, rows, mats, joints, count, block):
    b, g0, g1 = rows
    slots = b.shape[0]
    pos = lax.broadcasted_iota(jnp.int32, b.shape, 0)
    cut = pos >= count - 1
    for k in range(joints.shape[0]):
        cut = cut | (joints[k : k + 1, :] == (pos + 1) * block)
    k0, k1 = [lookup(conduct, comp, bit_masks(m.astype(jnp.int32))) for m in mats]
    link = jnp.where(cut, 0.0, SCALES[comp] * (k1 + roll(k0, -1)))
    wr = inverse(b + link + g1)
    lo, hi = b * wr, link * wr
    c = b * hi
    a = roll(c, 1)
    g = g0 + lo * g1 + roll(hi * g1, 1)
    steps = []
    s = 1
    while s < count:
        w = inverse(a + c + g)
        right, left = c * w, a * w
        steps.append((s, right, left))
        g_new = g + roll(right * g, s) + roll(left * g, -s)
        a, c, g = roll(right * a, s), roll(left * c, -s), g_new
        s *= 2
    return b, link, wr, lo, hi, steps, inverse(g)


def chain_source(structure, f0, f1):
    b, link, wr, lo, hi, steps, w = structure
    f = f0 + lo * f1 + roll(hi * f1, 1)
    for s, right, left in steps:
        f = f + roll(right * f, s) + roll(left * f, -s)
    x0 = f * w
    x1 = (f1 + b * x0 + link * roll(x0, -1)) * wr
    return x0, x1


def two_terms(x):
    coarse = x.astype(jnp.bfloat16)
    return coarse, (x - coarse.astype(jnp.float32)).astype(jnp.bfloat16)


def over(value, n):
    if n & (n - 1):
        return lax.div(value, n)
    return lax.shift_right_arithmetic(value, n.bit_length() - 1)


def low_first(me, n):
    return [k + over(k - me + n, n) for k in range(n - 1)]


def kernel(
    fields_in, material_in, conduct_in, joints_x_in, joints_y_in, half, advanced,
    fields, material, conduct, joints_x, joints_y,
    field_t, mat_t, half_t, resp_x, resp_y, part_y, mix, held_x, held_y, flow_y, ends,
    send_x, recv_x, send_y, recv_y, send_f, recv_f, load_sem,
):
    nx, ny = lax.axis_size("gx"), lax.axis_size("gy")
    mx, my = lax.axis_index("gx"), lax.axis_index("gy")
    rows, cols = material.shape
    loads = [
        pltpu.make_async_copy(source, target, load_sem.at[i])
        for i, (source, target) in enumerate(
            (
                (material_in, material),
                (conduct_in, conduct),
                (joints_x_in, joints_x),
                (fields_in, fields),
                (joints_y_in, joints_y),
            )
        )
    ]
    for load in loads:
        load.start()

    barrier = pltpu.get_barrier_semaphore()
    peers_x = low_first(mx, nx)
    peers_y = low_first(my, ny)
    for axis, peers in (("gx", peers_x), ("gy", peers_y)):
        for peer in peers:
            pl.semaphore_signal(
                barrier, inc=1, device_id={axis: peer}, device_id_type=pl.DeviceIdType.MESH
            )

    class Exchange:
        def __init__(self, axis, me, peers, held, slot, used, send, recv):
            self.axis, self.me, self.peers, self.held = axis, me, peers, held
            self.slot, self.used, self.send, self.recv = slot, used, send, recv
            self.slots = held.shape[0] // slot
            spare = self.slots - len(peers) - 1
            if spare > 0:
                held[(len(peers) + 1) * slot :, :] = jnp.ones(
                    (spare * slot, held.shape[1]), jnp.float32
                )

        def copy(self, k, owner):
            place = pl.multiple_of(owner * self.slot, self.slot)
            block = self.held.at[pl.ds(place, self.used), :]
            return pltpu.make_async_remote_copy(
                src_ref=block, dst_ref=block, send_sem=self.send.at[k],
                recv_sem=self.recv.at[owner], device_id={self.axis: self.peers[k]},
                device_id_type=pl.DeviceIdType.MESH,
            )

        def publish(self, lines):
            lines = list(lines) + [jnp.zeros_like(lines[0])] * (self.slot - len(lines))
            place = pl.multiple_of(self.me * self.slot, self.slot)
            self.held[pl.ds(place, self.slot), :] = jnp.concatenate(lines, axis=0)

        def start(self):
            for k in range(len(self.peers)):
                self.copy(k, self.me).start()

        def wait(self):
            for k, peer in enumerate(self.peers):
                self.copy(k, peer).wait_recv()

        def finish(self):
            for k in range(len(self.peers)):
                self.copy(k, self.me).wait_send()

        def item(self, q):
            return self.held[pl.ds(q, self.slots, stride=self.slot), :]

    ex_x = Exchange("gx", mx, peers_x, held_x, SLOT, ROWS, send_x, recv_x)
    ex_y = Exchange("gy", my, peers_y, held_y, SUB, SUB, send_y, recv_y)
    ex_f = Exchange("gy", my, peers_y, flow_y, SUB, 4, send_f, recv_f)

    def my_ends(comp, me, x0, x1):
        slots = x0.shape[0]
        base = 2 * comp * slots
        ends[pl.ds(base, slots), :] = x0
        ends[pl.ds(base + slots, slots), :] = x1
        return ends[pl.ds(me + base, 1), :], ends[pl.ds(me + base + slots, 1), :]

    for load in loads[:3]:
        load.wait()
    mat_t[...] = material[...].T
    jx = joints_x[...]
    span = cols // SUB
    along_x, mats = block_structure(conduct, mat_t, jx, mx * cols)
    loads[3].wait()
    for comp in range(2):
        field_t[comp] = fields[comp].T
    kept_x, lines = [], list(mats)
    for inner, shared in along_x:
        comp = len(kept_x)
        kept, f0, f1 = block_source(
            inner, [field_t[comp, pl.ds(t, SUB, stride=span), :] for t in range(span)]
        )
        kept_x.append(kept)
        lines += list(shared) + [f0, f1]
    ex_x.publish(lines)
    pl.semaphore_wait(barrier, nx + ny - 2)
    ex_x.start()

    loads[4].wait()
    jy = joints_y[...]
    span_y = rows // SUB
    along_y, mats = block_structure(conduct, material, jy, my * rows)
    ex_y.publish(list(mats) + list(along_y[0][1]) + list(along_y[1][1]))
    ex_y.start()

    zero = jnp.zeros((SUB, cols), jnp.float32)
    one = jnp.ones((SUB, cols), jnp.float32)
    none_x, none_y = ([zero] * span, zero), ([zero] * span_y, zero)

    def keep(ref, index, values):
        for t, value in enumerate(values):
            ref[index, pl.ds(t, SUB, stride=len(values)), :] = value

    for comp in range(2):
        inner = along_x[comp][0]
        for q, values in enumerate(
            (
                block_solve(inner, kept_x[comp], zero, zero),
                block_solve(inner, none_x, one, zero),
                block_solve(inner, none_x, zero, one),
            )
        ):
            keep(resp_x, 3 * comp + q, values)
        inner = along_y[comp][0]
        for q, values in enumerate(
            (block_solve(inner, none_y, one, zero), block_solve(inner, none_y, zero, one))
        ):
            keep(resp_y, 2 * comp + q, values)
    base = []
    for comp in range(2):
        turned = [resp_x[3 * comp + q].T for q in range(3)]
        for q in range(2):
            weight = resp_y[2 * comp + q]
            base.append(jnp.sum(weight * turned[0], axis=0, keepdims=True))
            for p in range(2):
                coarse, fine = two_terms(weight * turned[1 + p])
                at = (slice(p * rows, (p + 1) * rows), slice(q * cols, (q + 1) * cols))
                mix[comp, 0, *at] = coarse
                mix[comp, 1, *at] = fine

    ex_x.wait()
    mats = [ex_x.item(q) for q in range(2)]
    found_x, lines = [], []
    for comp in range(2):
        b, g0, g1, f0, f1 = [ex_x.item(2 + 5 * comp + q) for q in range(5)]
        structure = chain_structure(conduct, comp, (b, g0, g1), mats, jx, nx, cols)
        found = my_ends(comp, mx, *chain_source(structure, f0, f1))
        found_x.append(found)
        sides = jnp.concatenate(found, axis=1)
        coarse, fine = two_terms(sides)
        row = lax.broadcasted_iota(jnp.int32, (16, 2 * rows), 0)
        stack = jnp.where(row == 0, coarse.astype(jnp.float32), 0.0)
        stack = jnp.where(row == 1, fine.astype(jnp.float32), stack).astype(jnp.bfloat16)
        flow = sum(
            jnp.dot(stack, mix[comp, p], preferred_element_type=jnp.float32) for p in range(2)
        )
        flow = flow[0:1, :] + flow[1:2, :]
        for q in range(2):
            lines.append(base[2 * comp + q] + flow[:, q * cols : (q + 1) * cols])
    ex_f.publish(lines)
    ex_f.start()

    for comp in range(2):
        first, last = found_x[comp]
        half_t[comp] = (
            resp_x[3 * comp] + resp_x[3 * comp + 1] * first + resp_x[3 * comp + 2] * last
        )
        half[comp] = half_t[comp].T
        inner = along_y[comp][0]
        kept, _, _ = block_source(
            inner, [half[comp, pl.ds(t, SUB, stride=span_y), :] for t in range(span_y)]
        )
        keep(part_y, comp, block_solve(inner, kept, zero, zero))
    ex_y.wait()
    mats = [ex_y.item(q) for q in range(2)]
    structures = [
        chain_structure(
            conduct, comp, [ex_y.item(2 + 3 * comp + q) for q in range(3)], mats, jy, ny, rows
        )
        for comp in range(2)
    ]
    ex_f.wait()
    for comp in range(2):
        f0, f1 = [ex_f.item(2 * comp + q) for q in range(2)]
        first, last = my_ends(comp, my, *chain_source(structures[comp], f0, f1))
        advanced[comp] = (
            part_y[comp] + resp_y[2 * comp] * first + resp_y[2 * comp + 1] * last
        )
    ex_x.finish()
    ex_y.finish()
    ex_f.finish()


def write_out(half, advanced, half_out, advanced_out, sems):
    copies = [
        pltpu.make_async_copy(half, half_out, sems.at[0]),
        pltpu.make_async_copy(advanced, advanced_out, sems.at[1]),
    ]
    for copy in copies:
        copy.start()
    for copy in copies:
        copy.wait()


def per_device(nx, ny, fields, material, conduct, joints_x, joints_y):
    rows, cols = material.shape
    joints = joints_x.shape[1]
    vmem = pl.BlockSpec(memory_space=pltpu.VMEM)
    hbm = pl.BlockSpec(memory_space=pltpu.HBM)
    shape = jax.ShapeDtypeStruct(fields.shape, jnp.float32)
    sx, sy = max(nx, SUB), max(ny, SUB)
    solved = pl.pallas_call(
        kernel,
        out_shape=(shape, shape),
        in_specs=[hbm] * 5,
        out_specs=(vmem, vmem),
        scratch_shapes=[
            pltpu.VMEM((2, rows, cols), jnp.float32),
            pltpu.VMEM((rows, cols), jnp.int32),
            pltpu.SMEM(conduct.shape, jnp.float32),
            pltpu.VMEM((joints, rows), jnp.int32),
            pltpu.VMEM((joints, cols), jnp.int32),
            pltpu.VMEM((2, cols, rows), jnp.float32),
            pltpu.VMEM((cols, rows), jnp.int32),
            pltpu.VMEM((2, cols, rows), jnp.float32),
            pltpu.VMEM((6, cols, rows), jnp.float32),
            pltpu.VMEM((4, rows, cols), jnp.float32),
            pltpu.VMEM((2, rows, cols), jnp.float32),
            pltpu.VMEM((2, 2, 2 * rows, 2 * cols), jnp.bfloat16),
            pltpu.VMEM((sx * SLOT, rows), jnp.float32),
            pltpu.VMEM((sy * SUB, cols), jnp.float32),
            pltpu.VMEM((sy * SUB, cols), jnp.float32),
            pltpu.VMEM((4 * max(sx, sy), cols), jnp.float32),
            pltpu.SemaphoreType.DMA((nx,)),
            pltpu.SemaphoreType.DMA((nx,)),
            pltpu.SemaphoreType.DMA((ny,)),
            pltpu.SemaphoreType.DMA((ny,)),
            pltpu.SemaphoreType.DMA((ny,)),
            pltpu.SemaphoreType.DMA((ny,)),
            pltpu.SemaphoreType.DMA((5,)),
        ],
        compiler_params=pltpu.CompilerParams(
            collective_id=0, has_side_effects=True, vmem_limit_bytes=16 * 1024 * 1024
        ),
    )(
        *(
            pltpu.with_memory_space_constraint(x, pltpu.HBM)
            for x in (fields, material, conduct, joints_x.T, joints_y.T)
        )
    )
    return pl.pallas_call(
        write_out,
        out_shape=(shape, shape),
        in_specs=[vmem, vmem],
        out_specs=(hbm, hbm),
        scratch_shapes=[pltpu.SemaphoreType.DMA((2,))],
        compiler_params=pltpu.CompilerParams(vmem_limit_bytes=4 * 1024 * 1024),
    )(*solved)


def solution(mesh):
    return jax.shard_map(
        functools.partial(per_device, mesh.shape["gx"], mesh.shape["gy"]),
        mesh=mesh,
        in_specs=(P(None, "gy", "gx"), P("gy", "gx"), P(), P("gy", None), P("gx", None)),
        out_specs=(P(None, "gy", "gx"), P(None, "gy", "gx")),
        check_vma=False,
    )
```

```python
import functools

import jax
import jax.numpy as jnp
from jax import lax
from jax.experimental import pallas as pl
from jax.experimental.pallas import tpu as pltpu
from jax.sharding import PartitionSpec as P

MATERIALS = 8
FOURIER = 8192
DRYING = 4096
SCALES = (0.5 * FOURIER, 0.5 * DRYING)
SUB = 8
SLOT = 16
ROWS = 12


def inverse(x):
    guess = pl.reciprocal(x, approx=True)
    return guess * (2.0 - x * guess)


def lookup(conduct, comp, mats):
    low, mid, high = mats
    v = [conduct[comp, k] for k in range(MATERIALS)]
    pair = [jnp.where(low, v[2 * k + 1], v[2 * k]) for k in range(4)]
    quad = [jnp.where(mid, pair[2 * k + 1], pair[2 * k]) for k in range(2)]
    return jnp.where(high, quad[1], quad[0])


def bit_masks(mat):
    return (mat & 1) != 0, (mat & 2) != 0, (mat & 4) != 0


def fold(links, ground):
    ground = list(ground)
    index = list(range(len(ground)))
    plan = []
    while len(index) > 2:
        keep, merged = [index[0]], []
        p = 1
        while p < len(index):
            if p + 1 < len(index):
                a, k, b = index[p - 1 : p + 2]
                w = inverse(links[p - 1] + links[p] + ground[k])
                lo, hi = links[p - 1] * w, links[p] * w
                merged.append(links[p - 1] * hi)
                ground[a] = ground[a] + lo * ground[k]
                ground[b] = ground[b] + hi * ground[k]
                plan.append((a, k, b, lo, hi, w))
                keep.append(b)
                p += 2
            else:
                merged.append(links[p - 1])
                keep.append(index[p])
                p += 1
        index, links = keep, merged
    return plan, links[0], ground[0], ground[-1]


def fold_source(plan, source):
    source = list(source)
    for a, k, b, lo, hi, _ in plan:
        source[a] = source[a] + lo * source[k]
        source[b] = source[b] + hi * source[k]
    return source


def unfold(plan, source, first, last):
    x = {0: first, len(source) - 1: last}
    for a, k, b, lo, hi, w in reversed(plan):
        x[k] = source[k] * w + lo * x[a] + hi * x[b]
    return [x[k] for k in range(len(source))]


def roll(x, shift):
    return pltpu.roll(x, shift % x.shape[0], 0)


def block_structure(conduct, mat_ref, joints, base):
    span = mat_ref.shape[0] // SUB
    lane = mat_ref.shape[1]
    sub = lax.broadcasted_iota(jnp.int32, (SUB, lane), 0)
    bits = jnp.zeros((SUB, lane), jnp.int32)
    for k in range(joints.shape[0]):
        at = joints[k : k + 1, :] - base - sub * span
        bits = bits | jnp.where(
            (at >= 1) & (at <= span), jnp.left_shift(1, jnp.clip(at, 0, span)), 0
        )
    masks = []
    for t in range(span):
        last = mat_ref[pl.ds(t, SUB, stride=span), :]
        first = last if t == 0 else first
        masks.append(bit_masks(last))
    cut = [(bits & (1 << (t + 1))) != 0 for t in range(span)]
    out = []
    for comp in range(2):
        cond = [lookup(conduct, comp, m) for m in masks]
        after = cond[1:] + [roll(cond[0], -1)]
        face = [
            jnp.where(cut[t], 0.0, SCALES[comp] * (cond[t] + after[t])) for t in range(span)
        ]
        ones = jnp.ones((SUB, lane), jnp.float32)
        plan, b, gp, gq = fold(face[:-1], [ones] * span)
        link = jnp.where(sub == SUB - 1, 0.0, face[-1])
        wq = inverse(b + link + gq)
        lo = jnp.where(sub == SUB - 1, 0.0, b * wq)
        hi = link * wq
        c = jnp.where(sub == SUB - 1, b, b * hi)
        a = jnp.where(sub == 0, 0.0, roll(c, 1))
        g = gp + lo * gq + roll(hi * gq, 1)
        g_first = g
        steps = []
        s = 1
        while s < SUB:
            w = inverse(a + c + g)
            right = jnp.where((sub >= 1) & (sub <= SUB - 1 - s), c * w, 0.0)
            left = jnp.where(sub >= 1 + s, a * w, 0.0)
            steps.append((s, right, left))
            g_new = g + roll(right * g, s) + roll(left * g, -s)
            a_new = jnp.where(sub >= 1 + s, roll(right * a, s), a)
            c_new = jnp.where(sub <= SUB - 1 - s, roll(left * c, -s), c)
            a, c, g = a_new, c_new, g_new
            s *= 2
        w = inverse(a + c + g)
        aw, cw = a * w, c * w
        between = (aw * c)[1:2, :]
        ground0 = g_first[0:1, :] + (aw * g)[1:2, :]
        ground1 = (gq + cw * g)[SUB - 1 : SUB, :]
        inner = dict(
            plan=plan, b=b, link=link, wq=wq, lo=lo, hi=hi, steps=steps, w=w, aw=aw, cw=cw
        )
        out.append((inner, (between, ground0, ground1)))
    return out, (first[0:1, :].astype(jnp.float32), last[SUB - 1 : SUB, :].astype(jnp.float32))


def block_source(inner, source):
    source = fold_source(inner["plan"], source)
    fq = source[-1]
    f = source[0] + inner["lo"] * fq + roll(inner["hi"] * fq, 1)
    f_first = f
    for s, right, left in inner["steps"]:
        f = f + roll(right * f, s) + roll(left * f, -s)
    f0 = f_first[0:1, :] + (inner["aw"] * f)[1:2, :]
    f1 = (fq + inner["cw"] * f)[SUB - 1 : SUB, :]
    return (source, f), f0, f1


def block_solve(inner, kept, first, last):
    source, f = kept
    sub = lax.broadcasted_iota(jnp.int32, f.shape, 0)
    xp = f * inner["w"] + inner["aw"] * first + inner["cw"] * last
    xp = jnp.where(sub == 0, first, xp)
    xq = (source[-1] + inner["b"] * xp + inner["link"] * roll(xp, -1)) * inner["wq"]
    xq = jnp.where(sub == SUB - 1, last, xq)
    return unfold(inner["plan"], source, xp, xq)


def chain_structure(conduct, comp, rows, mats, joints, count, block):
    b, g0, g1 = rows
    slots = b.shape[0]
    pos = lax.broadcasted_iota(jnp.int32, b.shape, 0)
    cut = pos >= count - 1
    for k in range(joints.shape[0]):
        cut = cut | (joints[k : k + 1, :] == (pos + 1) * block)
    k0, k1 = [lookup(conduct, comp, bit_masks(m.astype(jnp.int32))) for m in mats]
    link = jnp.where(cut, 0.0, SCALES[comp] * (k1 + roll(k0, -1)))
    wr = inverse(b + link + g1)
    lo, hi = b * wr, link * wr
    c = b * hi
    a = roll(c, 1)
    g = g0 + lo * g1 + roll(hi * g1, 1)
    steps = []
    s = 1
    while s < count:
        w = inverse(a + c + g)
        right, left = c * w, a * w
        steps.append((s, right, left))
        g_new = g + roll(right * g, s) + roll(left * g, -s)
        a, c, g = roll(right * a, s), roll(left * c, -s), g_new
        s *= 2
    return b, link, wr, lo, hi, steps, inverse(g)


def chain_source(structure, f0, f1):
    b, link, wr, lo, hi, steps, w = structure
    f = f0 + lo * f1 + roll(hi * f1, 1)
    for s, right, left in steps:
        f = f + roll(right * f, s) + roll(left * f, -s)
    x0 = f * w
    x1 = (f1 + b * x0 + link * roll(x0, -1)) * wr
    return x0, x1


def two_terms(x):
    coarse = x.astype(jnp.bfloat16)
    return coarse, (x - coarse.astype(jnp.float32)).astype(jnp.bfloat16)


def over(value, n):
    if n & (n - 1):
        return lax.div(value, n)
    return lax.shift_right_arithmetic(value, n.bit_length() - 1)


def low_first(me, n):
    return [k + over(k - me + n, n) for k in range(n - 1)]


def kernel(
    fields_in, material_in, conduct_in, joints_x_in, joints_y_in, half, advanced,
    fields, material, conduct, joints_x, joints_y,
    field_t, mat_t, half_t, resp_x, resp_y, part_y, mix, held_x, held_y, flow_y, ends,
    send_x, recv_x, send_y, recv_y, send_f, recv_f, load_sem,
):
    nx, ny = lax.axis_size("gx"), lax.axis_size("gy")
    mx, my = lax.axis_index("gx"), lax.axis_index("gy")
    rows, cols = material.shape
    barrier = pltpu.get_barrier_semaphore()
    peers_x, peers_y = low_first(mx, nx), low_first(my, ny)

    def greet(axis, peers):
        for peer in peers:
            pl.semaphore_signal(
                barrier, inc=1, device_id={axis: peer}, device_id_type=pl.DeviceIdType.MESH
            )

    def load(sem, source, target):
        copy = pltpu.make_async_copy(source, target, load_sem.at[sem])
        copy.start()
        return copy

    greet("gx", peers_x)
    half_rows = rows // 2
    upper, lower = pl.ds(0, half_rows), pl.ds(half_rows, half_rows)
    early = [
        load(0, material_in.at[upper], material.at[upper]),
        load(1, material_in.at[lower], material.at[lower]),
        load(2, conduct_in, conduct),
        load(3, joints_x_in, joints_x),
    ]
    late = [load(4 + c, fields_in.at[c], fields.at[c]) for c in range(2)]
    last_load = load(6, joints_y_in, joints_y)
    greet("gy", peers_y)

    class Exchange:
        def __init__(self, axis, me, peers, held, slot, used, send, recv):
            self.axis, self.me, self.peers, self.held = axis, me, peers, held
            self.slot, self.used, self.send, self.recv = slot, used, send, recv
            self.slots = held.shape[0] // slot
            spare = self.slots - len(peers) - 1
            if spare > 0:
                held[(len(peers) + 1) * slot :, :] = jnp.ones(
                    (spare * slot, held.shape[1]), jnp.float32
                )

        def copy(self, k, owner):
            place = pl.multiple_of(owner * self.slot, self.slot)
            block = self.held.at[pl.ds(place, self.used), :]
            return pltpu.make_async_remote_copy(
                src_ref=block, dst_ref=block, send_sem=self.send.at[k],
                recv_sem=self.recv.at[owner], device_id={self.axis: self.peers[k]},
                device_id_type=pl.DeviceIdType.MESH,
            )

        def publish(self, lines):
            lines = list(lines) + [jnp.zeros_like(lines[0])] * (self.slot - len(lines))
            place = pl.multiple_of(self.me * self.slot, self.slot)
            self.held[pl.ds(place, self.slot), :] = jnp.concatenate(lines, axis=0)

        def start(self):
            for k in range(len(self.peers)):
                self.copy(k, self.me).start()

        def wait(self):
            for k, peer in enumerate(self.peers):
                self.copy(k, peer).wait_recv()

        def finish(self):
            for k in range(len(self.peers)):
                self.copy(k, self.me).wait_send()

        def item(self, q):
            return self.held[pl.ds(q, self.slots, stride=self.slot), :]

    ex_x = Exchange("gx", mx, peers_x, held_x, SLOT, ROWS, send_x, recv_x)
    ex_y = Exchange("gy", my, peers_y, held_y, SUB, SUB, send_y, recv_y)
    ex_f = Exchange("gy", my, peers_y, flow_y, SUB, 4, send_f, recv_f)

    def my_ends(comp, me, x0, x1):
        slots = x0.shape[0]
        base = 2 * comp * slots
        ends[pl.ds(base, slots), :] = x0
        ends[pl.ds(base + slots, slots), :] = x1
        return ends[pl.ds(me + base, 1), :], ends[pl.ds(me + base + slots, 1), :]

    for copy in early:
        copy.wait()
    mat_t[...] = material[...].T
    jx = joints_x[...]
    span = cols // SUB
    along_x, mats = block_structure(conduct, mat_t, jx, mx * cols)
    for comp in range(2):
        late[comp].wait()
        field_t[comp] = fields[comp].T
    kept_x, lines = [], list(mats)
    for inner, shared in along_x:
        comp = len(kept_x)
        kept, f0, f1 = block_source(
            inner, [field_t[comp, pl.ds(t, SUB, stride=span), :] for t in range(span)]
        )
        kept_x.append(kept)
        lines += list(shared) + [f0, f1]
    ex_x.publish(lines)
    pl.semaphore_wait(barrier, nx + ny - 2)
    ex_x.start()

    last_load.wait()
    jy = joints_y[...]
    span_y = rows // SUB
    along_y, mats = block_structure(conduct, material, jy, my * rows)
    ex_y.publish(list(mats) + list(along_y[0][1]) + list(along_y[1][1]))
    ex_y.start()

    zero = jnp.zeros((SUB, cols), jnp.float32)
    one = jnp.ones((SUB, cols), jnp.float32)
    none_x, none_y = ([zero] * span, zero), ([zero] * span_y, zero)

    def keep(ref, index, values):
        for t, value in enumerate(values):
            ref[index, pl.ds(t, SUB, stride=len(values)), :] = value

    for comp in range(2):
        inner = along_x[comp][0]
        for q, values in enumerate(
            (
                block_solve(inner, kept_x[comp], zero, zero),
                block_solve(inner, none_x, one, zero),
                block_solve(inner, none_x, zero, one),
            )
        ):
            keep(resp_x, 3 * comp + q, values)
        inner = along_y[comp][0]
        for q, values in enumerate(
            (block_solve(inner, none_y, one, zero), block_solve(inner, none_y, zero, one))
        ):
            keep(resp_y, 2 * comp + q, values)
    base = []
    for comp in range(2):
        turned = [resp_x[3 * comp + q].T for q in range(3)]
        for q in range(2):
            weight = resp_y[2 * comp + q]
            base.append(jnp.sum(weight * turned[0], axis=0, keepdims=True))
            for p in range(2):
                coarse, fine = two_terms(weight * turned[1 + p])
                at = (slice(p * rows, (p + 1) * rows), slice(q * cols, (q + 1) * cols))
                mix[comp, 0, *at] = coarse
                mix[comp, 1, *at] = fine

    ex_x.wait()
    mats = [ex_x.item(q) for q in range(2)]
    found_x, lines = [], []
    for comp in range(2):
        b, g0, g1, f0, f1 = [ex_x.item(2 + 5 * comp + q) for q in range(5)]
        structure = chain_structure(conduct, comp, (b, g0, g1), mats, jx, nx, cols)
        found = my_ends(comp, mx, *chain_source(structure, f0, f1))
        found_x.append(found)
        sides = jnp.concatenate(found, axis=1)
        coarse, fine = two_terms(sides)
        row = lax.broadcasted_iota(jnp.int32, (16, 2 * rows), 0)
        stack = jnp.where(row == 0, coarse.astype(jnp.float32), 0.0)
        stack = jnp.where(row == 1, fine.astype(jnp.float32), stack).astype(jnp.bfloat16)
        flow = sum(
            jnp.dot(stack, mix[comp, p], preferred_element_type=jnp.float32) for p in range(2)
        )
        flow = flow[0:1, :] + flow[1:2, :]
        for q in range(2):
            lines.append(base[2 * comp + q] + flow[:, q * cols : (q + 1) * cols])
    ex_f.publish(lines)
    ex_f.start()

    for comp in range(2):
        first, last = found_x[comp]
        half_t[comp] = (
            resp_x[3 * comp] + resp_x[3 * comp + 1] * first + resp_x[3 * comp + 2] * last
        )
        half[comp] = half_t[comp].T
        inner = along_y[comp][0]
        kept, _, _ = block_source(
            inner, [half[comp, pl.ds(t, SUB, stride=span_y), :] for t in range(span_y)]
        )
        keep(part_y, comp, block_solve(inner, kept, zero, zero))
    ex_y.wait()
    mats = [ex_y.item(q) for q in range(2)]
    structures = [
        chain_structure(
            conduct, comp, [ex_y.item(2 + 3 * comp + q) for q in range(3)], mats, jy, ny, rows
        )
        for comp in range(2)
    ]
    ex_f.wait()
    for comp in range(2):
        f0, f1 = [ex_f.item(2 * comp + q) for q in range(2)]
        first, last = my_ends(comp, my, *chain_source(structures[comp], f0, f1))
        advanced[comp] = (
            part_y[comp] + resp_y[2 * comp] * first + resp_y[2 * comp + 1] * last
        )
    ex_x.finish()
    ex_y.finish()
    ex_f.finish()


def write_out(half, advanced, half_out, advanced_out, sems):
    copies = [
        pltpu.make_async_copy(half, half_out, sems.at[0]),
        pltpu.make_async_copy(advanced, advanced_out, sems.at[1]),
    ]
    for copy in copies:
        copy.start()
    for copy in copies:
        copy.wait()


def per_device(nx, ny, fields, material, conduct, joints_x, joints_y):
    rows, cols = material.shape
    joints = joints_x.shape[1]
    vmem = pl.BlockSpec(memory_space=pltpu.VMEM)
    hbm = pl.BlockSpec(memory_space=pltpu.HBM)
    shape = jax.ShapeDtypeStruct(fields.shape, jnp.float32)
    sx, sy = max(nx, SUB), max(ny, SUB)
    solved = pl.pallas_call(
        kernel,
        out_shape=(shape, shape),
        in_specs=[hbm] * 5,
        out_specs=(vmem, vmem),
        scratch_shapes=[
            pltpu.VMEM((2, rows, cols), jnp.float32),
            pltpu.VMEM((rows, cols), jnp.int32),
            pltpu.SMEM(conduct.shape, jnp.float32),
            pltpu.VMEM((joints, rows), jnp.int32),
            pltpu.VMEM((joints, cols), jnp.int32),
            pltpu.VMEM((2, cols, rows), jnp.float32),
            pltpu.VMEM((cols, rows), jnp.int32),
            pltpu.VMEM((2, cols, rows), jnp.float32),
            pltpu.VMEM((6, cols, rows), jnp.float32),
            pltpu.VMEM((4, rows, cols), jnp.float32),
            pltpu.VMEM((2, rows, cols), jnp.float32),
            pltpu.VMEM((2, 2, 2 * rows, 2 * cols), jnp.bfloat16),
            pltpu.VMEM((sx * SLOT, rows), jnp.float32),
            pltpu.VMEM((sy * SUB, cols), jnp.float32),
            pltpu.VMEM((sy * SUB, cols), jnp.float32),
            pltpu.VMEM((4 * max(sx, sy), cols), jnp.float32),
            pltpu.SemaphoreType.DMA((nx,)),
            pltpu.SemaphoreType.DMA((nx,)),
            pltpu.SemaphoreType.DMA((ny,)),
            pltpu.SemaphoreType.DMA((ny,)),
            pltpu.SemaphoreType.DMA((ny,)),
            pltpu.SemaphoreType.DMA((ny,)),
            pltpu.SemaphoreType.DMA((7,)),
        ],
        compiler_params=pltpu.CompilerParams(
            collective_id=0, has_side_effects=True, vmem_limit_bytes=16 * 1024 * 1024
        ),
    )(
        *(
            pltpu.with_memory_space_constraint(x, pltpu.HBM)
            for x in (fields, material, conduct, joints_x.T, joints_y.T)
        )
    )
    return pl.pallas_call(
        write_out,
        out_shape=(shape, shape),
        in_specs=[vmem, vmem],
        out_specs=(hbm, hbm),
        scratch_shapes=[pltpu.SemaphoreType.DMA((2,))],
        compiler_params=pltpu.CompilerParams(vmem_limit_bytes=4 * 1024 * 1024),
    )(*solved)


def solution(mesh):
    return jax.shard_map(
        functools.partial(per_device, mesh.shape["gx"], mesh.shape["gy"]),
        mesh=mesh,
        in_specs=(P(None, "gy", "gx"), P("gy", "gx"), P(), P("gy", None), P("gx", None)),
        out_specs=(P(None, "gy", "gx"), P(None, "gy", "gx")),
        check_vma=False,
    )
```

```python
import functools

import jax
import jax.numpy as jnp
from jax import lax
from jax.experimental import pallas as pl
from jax.experimental.pallas import tpu as pltpu
from jax.sharding import PartitionSpec as P

MATERIALS = 8
FOURIER = 8192
DRYING = 4096
SCALES = (0.5 * FOURIER, 0.5 * DRYING)
SUB = 8
SLOT = 16
ROWS = 12


def inverse(x):
    guess = pl.reciprocal(x, approx=True)
    return guess * (2.0 - x * guess)


def lookup(conduct, comp, mats):
    low, mid, high = mats
    v = [conduct[comp, k] for k in range(MATERIALS)]
    pair = [jnp.where(low, v[2 * k + 1], v[2 * k]) for k in range(4)]
    quad = [jnp.where(mid, pair[2 * k + 1], pair[2 * k]) for k in range(2)]
    return jnp.where(high, quad[1], quad[0])


def bit_masks(mat):
    return (mat & 1) != 0, (mat & 2) != 0, (mat & 4) != 0


def fold(links, ground):
    ground = list(ground)
    index = list(range(len(ground)))
    plan = []
    while len(index) > 2:
        keep, merged = [index[0]], []
        p = 1
        while p < len(index):
            if p + 1 < len(index):
                a, k, b = index[p - 1 : p + 2]
                w = inverse(links[p - 1] + links[p] + ground[k])
                lo, hi = links[p - 1] * w, links[p] * w
                merged.append(links[p - 1] * hi)
                ground[a] = ground[a] + lo * ground[k]
                ground[b] = ground[b] + hi * ground[k]
                plan.append((a, k, b, lo, hi, w))
                keep.append(b)
                p += 2
            else:
                merged.append(links[p - 1])
                keep.append(index[p])
                p += 1
        index, links = keep, merged
    return plan, links[0], ground[0], ground[-1]


def fold_source(plan, source):
    source = list(source)
    for a, k, b, lo, hi, _ in plan:
        source[a] = source[a] + lo * source[k]
        source[b] = source[b] + hi * source[k]
    return source


def unfold(plan, source, first, last):
    x = {0: first, len(source) - 1: last}
    for a, k, b, lo, hi, w in reversed(plan):
        x[k] = source[k] * w + lo * x[a] + hi * x[b]
    return [x[k] for k in range(len(source))]


def roll(x, shift):
    return pltpu.roll(x, shift % x.shape[0], 0)


def block_structure(conduct, mat_ref, joints, base):
    span = mat_ref.shape[0] // SUB
    lane = mat_ref.shape[1]
    sub = lax.broadcasted_iota(jnp.int32, (SUB, lane), 0)
    bits = jnp.zeros((SUB, lane), jnp.int32)
    for k in range(joints.shape[0]):
        at = joints[k : k + 1, :] - base - sub * span
        bits = bits | jnp.where(
            (at >= 1) & (at <= span), jnp.left_shift(1, jnp.clip(at, 0, span)), 0
        )
    masks = []
    for t in range(span):
        last = mat_ref[pl.ds(t, SUB, stride=span), :]
        first = last if t == 0 else first
        masks.append(bit_masks(last))
    cut = [(bits & (1 << (t + 1))) != 0 for t in range(span)]
    out = []
    for comp in range(2):
        cond = [lookup(conduct, comp, m) for m in masks]
        after = cond[1:] + [roll(cond[0], -1)]
        face = [
            jnp.where(cut[t], 0.0, SCALES[comp] * (cond[t] + after[t])) for t in range(span)
        ]
        ones = jnp.ones((SUB, lane), jnp.float32)
        plan, b, gp, gq = fold(face[:-1], [ones] * span)
        link = jnp.where(sub == SUB - 1, 0.0, face[-1])
        wq = inverse(b + link + gq)
        lo = jnp.where(sub == SUB - 1, 0.0, b * wq)
        hi = link * wq
        c = jnp.where(sub == SUB - 1, b, b * hi)
        a = jnp.where(sub == 0, 0.0, roll(c, 1))
        g = gp + lo * gq + roll(hi * gq, 1)
        g_first = g
        steps = []
        s = 1
        while s < SUB:
            w = inverse(a + c + g)
            right = jnp.where((sub >= 1) & (sub <= SUB - 1 - s), c * w, 0.0)
            left = jnp.where(sub >= 1 + s, a * w, 0.0)
            steps.append((s, right, left))
            g_new = g + roll(right * g, s) + roll(left * g, -s)
            a_new = jnp.where(sub >= 1 + s, roll(right * a, s), a)
            c_new = jnp.where(sub <= SUB - 1 - s, roll(left * c, -s), c)
            a, c, g = a_new, c_new, g_new
            s *= 2
        w = inverse(a + c + g)
        aw, cw = a * w, c * w
        between = (aw * c)[1:2, :]
        ground0 = g_first[0:1, :] + (aw * g)[1:2, :]
        ground1 = (gq + cw * g)[SUB - 1 : SUB, :]
        inner = dict(
            plan=plan, b=b, link=link, wq=wq, lo=lo, hi=hi, steps=steps, w=w, aw=aw, cw=cw
        )
        out.append((inner, (between, ground0, ground1)))
    return out, (first[0:1, :].astype(jnp.float32), last[SUB - 1 : SUB, :].astype(jnp.float32))


def block_source(inner, source):
    source = fold_source(inner["plan"], source)
    fq = source[-1]
    f = source[0] + inner["lo"] * fq + roll(inner["hi"] * fq, 1)
    f_first = f
    for s, right, left in inner["steps"]:
        f = f + roll(right * f, s) + roll(left * f, -s)
    f0 = f_first[0:1, :] + (inner["aw"] * f)[1:2, :]
    f1 = (fq + inner["cw"] * f)[SUB - 1 : SUB, :]
    return (source, f), f0, f1


def block_solve(inner, kept, first, last):
    source, f = kept
    sub = lax.broadcasted_iota(jnp.int32, f.shape, 0)
    xp = f * inner["w"] + inner["aw"] * first + inner["cw"] * last
    xp = jnp.where(sub == 0, first, xp)
    xq = (source[-1] + inner["b"] * xp + inner["link"] * roll(xp, -1)) * inner["wq"]
    xq = jnp.where(sub == SUB - 1, last, xq)
    return unfold(inner["plan"], source, xp, xq)


def chain_structure(conduct, comp, rows, mats, joints, count, block):
    b, g0, g1 = rows
    slots = b.shape[0]
    pos = lax.broadcasted_iota(jnp.int32, b.shape, 0)
    cut = pos >= count - 1
    for k in range(joints.shape[0]):
        cut = cut | (joints[k : k + 1, :] == (pos + 1) * block)
    k0, k1 = [lookup(conduct, comp, bit_masks(m.astype(jnp.int32))) for m in mats]
    link = jnp.where(cut, 0.0, SCALES[comp] * (k1 + roll(k0, -1)))
    wr = inverse(b + link + g1)
    lo, hi = b * wr, link * wr
    c = b * hi
    a = roll(c, 1)
    g = g0 + lo * g1 + roll(hi * g1, 1)
    steps = []
    s = 1
    while s < count:
        w = inverse(a + c + g)
        right, left = c * w, a * w
        steps.append((s, right, left))
        g_new = g + roll(right * g, s) + roll(left * g, -s)
        a, c, g = roll(right * a, s), roll(left * c, -s), g_new
        s *= 2
    return b, link, wr, lo, hi, steps, inverse(g)


def chain_source(structure, f0, f1):
    b, link, wr, lo, hi, steps, w = structure
    f = f0 + lo * f1 + roll(hi * f1, 1)
    for s, right, left in steps:
        f = f + roll(right * f, s) + roll(left * f, -s)
    x0 = f * w
    x1 = (f1 + b * x0 + link * roll(x0, -1)) * wr
    return x0, x1


def two_terms(x):
    coarse = x.astype(jnp.bfloat16)
    return coarse, (x - coarse.astype(jnp.float32)).astype(jnp.bfloat16)


def over(value, n):
    if n & (n - 1):
        return lax.div(value, n)
    return lax.shift_right_arithmetic(value, n.bit_length() - 1)


def low_first(me, n):
    return [k + over(k - me + n, n) for k in range(n - 1)]


def kernel(
    fields_in, material_in, conduct_in, joints_x_in, joints_y_in, half, advanced,
    fields, material, conduct, joints_x, joints_y,
    field_t, mat_t, half_t, resp_x, resp_y, part_y, mix, saved, base, held_x, held_y, flow_y, ends,
    send_x, recv_x, send_y, recv_y, send_f, recv_f, load_sem,
):
    nx, ny = lax.axis_size("gx"), lax.axis_size("gy")
    mx, my = lax.axis_index("gx"), lax.axis_index("gy")
    rows, cols = material.shape
    loads = [
        pltpu.make_async_copy(source, target, load_sem.at[i])
        for i, (source, target) in enumerate(
            (
                (material_in, material),
                (conduct_in, conduct),
                (joints_x_in, joints_x),
                (fields_in, fields),
                (joints_y_in, joints_y),
            )
        )
    ]
    for load in loads:
        load.start()

    barrier = pltpu.get_barrier_semaphore()
    peers_x = low_first(mx, nx)
    peers_y = low_first(my, ny)
    for axis, peers in (("gx", peers_x), ("gy", peers_y)):
        for peer in peers:
            pl.semaphore_signal(
                barrier, inc=1, device_id={axis: peer}, device_id_type=pl.DeviceIdType.MESH
            )

    class Exchange:
        def __init__(self, axis, me, peers, held, slot, used, send, recv):
            self.axis, self.me, self.peers, self.held = axis, me, peers, held
            self.slot, self.used, self.send, self.recv = slot, used, send, recv
            self.slots = held.shape[0] // slot
            spare = self.slots - len(peers) - 1
            if spare > 0:
                held[(len(peers) + 1) * slot :, :] = jnp.ones(
                    (spare * slot, held.shape[1]), jnp.float32
                )

        def copy(self, k, owner):
            place = pl.multiple_of(owner * self.slot, self.slot)
            block = self.held.at[pl.ds(place, self.used), :]
            return pltpu.make_async_remote_copy(
                src_ref=block, dst_ref=block, send_sem=self.send.at[k],
                recv_sem=self.recv.at[owner], device_id={self.axis: self.peers[k]},
                device_id_type=pl.DeviceIdType.MESH,
            )

        def publish(self, lines):
            lines = list(lines) + [jnp.zeros_like(lines[0])] * (self.slot - len(lines))
            place = pl.multiple_of(self.me * self.slot, self.slot)
            self.held[pl.ds(place, self.slot), :] = jnp.concatenate(lines, axis=0)

        def start(self):
            for k in range(len(self.peers)):
                self.copy(k, self.me).start()

        def wait(self):
            for k, peer in enumerate(self.peers):
                self.copy(k, peer).wait_recv()

        def finish(self):
            for k in range(len(self.peers)):
                self.copy(k, self.me).wait_send()

        def item(self, q):
            return self.held[pl.ds(q, self.slots, stride=self.slot), :]

    ex_x = Exchange("gx", mx, peers_x, held_x, SLOT, ROWS, send_x, recv_x)
    ex_y = Exchange("gy", my, peers_y, held_y, SUB, SUB, send_y, recv_y)
    ex_f = Exchange("gy", my, peers_y, flow_y, SUB, 4, send_f, recv_f)

    def my_ends(comp, me, x0, x1):
        slots = x0.shape[0]
        base = 2 * comp * slots
        ends[pl.ds(base, slots), :] = x0
        ends[pl.ds(base + slots, slots), :] = x1
        return ends[pl.ds(me + base, 1), :], ends[pl.ds(me + base + slots, 1), :]

    for load in loads[:3]:
        load.wait()
    mat_t[...] = material[...].T
    jx = joints_x[...]
    span = cols // SUB
    along_x, mats = block_structure(conduct, mat_t, jx, mx * cols)
    loads[3].wait()
    for comp in range(2):
        field_t[comp] = fields[comp].T
    kept_x, lines = [], list(mats)
    for inner, shared in along_x:
        comp = len(kept_x)
        kept, f0, f1 = block_source(
            inner, [field_t[comp, pl.ds(t, SUB, stride=span), :] for t in range(span)]
        )
        kept_x.append(kept)
        lines += list(shared) + [f0, f1]
    ex_x.publish(lines)
    loads[4].wait()
    jy = joints_y[...]
    span_y = rows // SUB
    zero = jnp.zeros((SUB, cols), jnp.float32)
    one = jnp.ones((SUB, cols), jnp.float32)
    static = {}

    def keep(ref, index, values):
        for t, value in enumerate(values):
            ref[index, pl.ds(t, SUB, stride=len(values)), :] = value

    def prepare():
        along_y, mats = block_structure(conduct, material, jy, my * rows)
        ex_y.publish(list(mats) + list(along_y[0][1]) + list(along_y[1][1]))

        none_x, none_y = ([zero] * span, zero), ([zero] * span_y, zero)

        for comp in range(2):
            inner = along_x[comp][0]
            for q, values in enumerate(
                (
                    block_solve(inner, kept_x[comp], zero, zero),
                    block_solve(inner, none_x, one, zero),
                    block_solve(inner, none_x, zero, one),
                )
            ):
                keep(resp_x, 3 * comp + q, values)
            inner = along_y[comp][0]
            for q, values in enumerate(
                (block_solve(inner, none_y, one, zero), block_solve(inner, none_y, zero, one))
            ):
                keep(resp_y, 2 * comp + q, values)
        flat, kind = jax.tree.flatten([inner for inner, _ in along_y])
        static.update(kind=kind, leaves=[x if isinstance(x, int) else None for x in flat])
        for at, leaf in enumerate(flat):
            if not isinstance(leaf, int):
                saved[at] = leaf
        for comp in range(2):
            turned = [resp_x[3 * comp + q].T for q in range(3)]
            for q in range(2):
                weight = resp_y[2 * comp + q]
                base[2 * comp + q : 2 * comp + q + 1, :] = jnp.sum(
                    weight * turned[0], axis=0, keepdims=True
                )
                for p in range(2):
                    coarse, fine = two_terms(weight * turned[1 + p])
                    spot = (slice(p * rows, (p + 1) * rows), slice(q * cols, (q + 1) * cols))
                    mix[comp, 0, *spot] = coarse
                    mix[comp, 1, *spot] = fine


    def send():
        pl.semaphore_wait(barrier, nx + ny - 2)
        ex_x.start()

    late = over(2 * mx, nx)

    def turn(step, carry):
        pl.when(step == late)(prepare)
        pl.when(step == 1 - late)(send)
        return carry

    lax.fori_loop(0, 2, turn, 0)
    ex_y.start()
    leaves = [saved[at] if x is None else x for at, x in enumerate(static["leaves"])]
    inner_y = jax.tree.unflatten(static["kind"], leaves)

    ex_x.wait()
    mats = [ex_x.item(q) for q in range(2)]
    found_x, lines = [], []
    for comp in range(2):
        b, g0, g1, f0, f1 = [ex_x.item(2 + 5 * comp + q) for q in range(5)]
        structure = chain_structure(conduct, comp, (b, g0, g1), mats, jx, nx, cols)
        found = my_ends(comp, mx, *chain_source(structure, f0, f1))
        found_x.append(found)
        sides = jnp.concatenate(found, axis=1)
        coarse, fine = two_terms(sides)
        row = lax.broadcasted_iota(jnp.int32, (16, 2 * rows), 0)
        stack = jnp.where(row == 0, coarse.astype(jnp.float32), 0.0)
        stack = jnp.where(row == 1, fine.astype(jnp.float32), stack).astype(jnp.bfloat16)
        flow = sum(
            jnp.dot(stack, mix[comp, p], preferred_element_type=jnp.float32) for p in range(2)
        )
        flow = flow[0:1, :] + flow[1:2, :]
        for q in range(2):
            lines.append(base[2 * comp + q : 2 * comp + q + 1, :] + flow[:, q * cols : (q + 1) * cols])
    ex_f.publish(lines)
    ex_f.start()

    for comp in range(2):
        first, last = found_x[comp]
        half_t[comp] = (
            resp_x[3 * comp] + resp_x[3 * comp + 1] * first + resp_x[3 * comp + 2] * last
        )
        half[comp] = half_t[comp].T
        inner = inner_y[comp]
        kept, _, _ = block_source(
            inner, [half[comp, pl.ds(t, SUB, stride=span_y), :] for t in range(span_y)]
        )
        keep(part_y, comp, block_solve(inner, kept, zero, zero))
    ex_y.wait()
    mats = [ex_y.item(q) for q in range(2)]
    structures = [
        chain_structure(
            conduct, comp, [ex_y.item(2 + 3 * comp + q) for q in range(3)], mats, jy, ny, rows
        )
        for comp in range(2)
    ]
    ex_f.wait()
    for comp in range(2):
        f0, f1 = [ex_f.item(2 * comp + q) for q in range(2)]
        first, last = my_ends(comp, my, *chain_source(structures[comp], f0, f1))
        advanced[comp] = (
            part_y[comp] + resp_y[2 * comp] * first + resp_y[2 * comp + 1] * last
        )
    ex_x.finish()
    ex_y.finish()
    ex_f.finish()


def write_out(half, advanced, half_out, advanced_out, sems):
    copies = [
        pltpu.make_async_copy(half, half_out, sems.at[0]),
        pltpu.make_async_copy(advanced, advanced_out, sems.at[1]),
    ]
    for copy in copies:
        copy.start()
    for copy in copies:
        copy.wait()


def per_device(nx, ny, fields, material, conduct, joints_x, joints_y):
    rows, cols = material.shape
    joints = joints_x.shape[1]
    vmem = pl.BlockSpec(memory_space=pltpu.VMEM)
    hbm = pl.BlockSpec(memory_space=pltpu.HBM)
    shape = jax.ShapeDtypeStruct(fields.shape, jnp.float32)
    sx, sy = max(nx, SUB), max(ny, SUB)
    solved = pl.pallas_call(
        kernel,
        out_shape=(shape, shape),
        in_specs=[hbm] * 5,
        out_specs=(vmem, vmem),
        scratch_shapes=[
            pltpu.VMEM((2, rows, cols), jnp.float32),
            pltpu.VMEM((rows, cols), jnp.int32),
            pltpu.SMEM(conduct.shape, jnp.float32),
            pltpu.VMEM((joints, rows), jnp.int32),
            pltpu.VMEM((joints, cols), jnp.int32),
            pltpu.VMEM((2, cols, rows), jnp.float32),
            pltpu.VMEM((cols, rows), jnp.int32),
            pltpu.VMEM((2, cols, rows), jnp.float32),
            pltpu.VMEM((6, cols, rows), jnp.float32),
            pltpu.VMEM((4, rows, cols), jnp.float32),
            pltpu.VMEM((2, rows, cols), jnp.float32),
            pltpu.VMEM((2, 2, 2 * rows, 2 * cols), jnp.bfloat16),
            pltpu.VMEM((256, SUB, cols), jnp.float32),
            pltpu.VMEM((SUB, cols), jnp.float32),
            pltpu.VMEM((sx * SLOT, rows), jnp.float32),
            pltpu.VMEM((sy * SUB, cols), jnp.float32),
            pltpu.VMEM((sy * SUB, cols), jnp.float32),
            pltpu.VMEM((4 * max(sx, sy), cols), jnp.float32),
            pltpu.SemaphoreType.DMA((nx,)),
            pltpu.SemaphoreType.DMA((nx,)),
            pltpu.SemaphoreType.DMA((ny,)),
            pltpu.SemaphoreType.DMA((ny,)),
            pltpu.SemaphoreType.DMA((ny,)),
            pltpu.SemaphoreType.DMA((ny,)),
            pltpu.SemaphoreType.DMA((5,)),
        ],
        compiler_params=pltpu.CompilerParams(
            collective_id=0, has_side_effects=True, vmem_limit_bytes=16 * 1024 * 1024
        ),
    )(
        *(
            pltpu.with_memory_space_constraint(x, pltpu.HBM)
            for x in (fields, material, conduct, joints_x.T, joints_y.T)
        )
    )
    return pl.pallas_call(
        write_out,
        out_shape=(shape, shape),
        in_specs=[vmem, vmem],
        out_specs=(hbm, hbm),
        scratch_shapes=[pltpu.SemaphoreType.DMA((2,))],
        compiler_params=pltpu.CompilerParams(vmem_limit_bytes=4 * 1024 * 1024),
    )(*solved)


def solution(mesh):
    return jax.shard_map(
        functools.partial(per_device, mesh.shape["gx"], mesh.shape["gy"]),
        mesh=mesh,
        in_specs=(P(None, "gy", "gx"), P("gy", "gx"), P(), P("gy", None), P("gx", None)),
        out_specs=(P(None, "gy", "gx"), P(None, "gy", "gx")),
        check_vma=False,
    )
```
